256 devices in a mesh: grp: 32 (over y, z), seq: 8 (over x, core).
Axes of the slice: x: 4, y: 4, z: 8, core: 2. Of those that a mesh axis runs over, the one named last changes fastest.
Arguments:
- queries: bfloat16 [65536, 1280], P(('grp', 'seq')), may hold values from -24 to 24
- key_rows: bfloat16 [65536, 1280], P(('grp', 'seq')), may hold values from -24 to 24
- values: bfloat16 [65536, 1280], P(('grp', 'seq')), may hold values from -6 to 6
- segment_ids: int32 [65536], P(('grp', 'seq')), may hold values from 0 to 511, as said below
- merger_norm_gain: float32 [1280], replicated, may hold values from 0.5 to 1.5
- merge_weight: bfloat16 [5120, 8192], P('grp', 'seq'), may hold values from -0.078125 to 0.078125
- text_rows: bfloat16 [32768, 8192], P(('grp', 'seq')), may hold values from -6 to 6
- token_gain: float32 [8192], replicated, may hold values from 0.5 to 1.5
- cotangent: bfloat16 [32768, 8192], P(('grp', 'seq')), may hold values from -6 to 6
- send_slot: int32 [16384], P(('grp', 'seq')), may hold values from 0 to 63, as said below
- place_pos: int32 [16384], P(('grp', 'seq')), may hold values from 0 to 127, as said below
Outputs:
- hidden: bfloat16 [32768, 8192], P(('grp', 'seq'))
- vision_output_gradient: bfloat16 [65536, 1280], P(('grp', 'seq'))
The draws below stay inside these ranges and needn't reach their ends.
Inputs may be any that keep to these rules, and one draw needn't show every extreme that they name: `segment_ids`: ids are never smaller than the previous patch's within a group of 2048 patches; patches of one image share an id and come in runs whose length is a multiple of 4; image sizes differ from group to group. `send_slot`: within each device's 64 rows a permutation of 0 to 63; slot c goes to language replica c // 2. `place_pos`: within each device's 64 entries all positions differ.
All inputs are finite; a program needn't handle non-finite values.
Results may differ from the reference program's by a relative error of at most 0.019.
Values may be sent and summed in bfloat16 or wider, within the bound.
A program may use at most 128 MiB of HBM per device.

```python
import jax
import jax.numpy as jnp
from jax import lax

VISION_WIDTH = 1280
HEADS = 16
D = 8192
HEAD_DIM = 80
MERGER_FEATURES = 5120
VT_DEV = 256
TOK_DEV = 128
DEVICE_VIS_ROWS = 64
SLOT_ROWS = 2
VTOKENS = 65536
TOTAL_VIS_ROWS = 16384
TOKENS = 32768
N_SEQ = 8


def draw_queries(key, part):
    key = jax.random.fold_in(key, 11)
    drawn = jnp.clip(jax.random.normal(key, (VTOKENS, VISION_WIDTH), jnp.float32), -4.0, 4.0)
    return drawn.astype(jnp.bfloat16)


def draw_key_rows(key, part):
    key = jax.random.fold_in(key, 12)
    drawn = jnp.clip(jax.random.normal(key, (VTOKENS, VISION_WIDTH), jnp.float32), -4.0, 4.0)
    return drawn.astype(jnp.bfloat16)


def draw_segment_ids(key, part):
    key = jax.random.fold_in(key, 21)
    units = VT_DEV * N_SEQ // 4
    groups = VTOKENS // (4 * units)
    first_key, second_key = jax.random.split(key)
    exponents = jax.random.randint(first_key, (groups, 1), 3, 8)
    raw_bits = jax.random.randint(second_key, (groups, units), 0, 1 << 20)
    period = jnp.left_shift(jnp.int32(1), exponents)
    unit_index = jnp.arange(units, dtype=jnp.int32)
    starts_here = (raw_bits % period == 0) | (unit_index == 0)[None, :] | (unit_index == units - 1)[None, :]
    starts = lax.cummax(jnp.where(starts_here, unit_index[None, :], 0), axis=1)
    return jnp.repeat(starts, 4, axis=1).reshape(-1).astype(jnp.int32)


def permute_one(one_key):
    return jax.random.permutation(one_key, DEVICE_VIS_ROWS)


def positions_one(one_key):
    return jax.random.permutation(one_key, TOK_DEV)[:DEVICE_VIS_ROWS]


def draw_send_slot(key, part):
    key = jax.random.fold_in(key, 31)
    device_keys = jax.random.split(key, TOTAL_VIS_ROWS // DEVICE_VIS_ROWS)
    return jax.vmap(permute_one)(device_keys).reshape(-1).astype(jnp.int32)


def draw_place_pos(key, part):
    key = jax.random.fold_in(key, 41)
    device_keys = jax.random.split(key, TOTAL_VIS_ROWS // DEVICE_VIS_ROWS)
    return jax.vmap(positions_one)(device_keys).reshape(-1).astype(jnp.int32)


def level_of(own_key, extent, pieces, least, top_value):
    def one(position, parts):
        draws = jax.random.uniform(jax.random.fold_in(jax.random.fold_in(own_key, 6), position), (parts,), jnp.float32, least / len(pieces), top_value / len(pieces))
        return jnp.repeat(jnp.exp(draws), extent[position] // parts).reshape((-1,) + (1,) * (len(extent) - position - 1))

    gain = one(*pieces[0])
    for cut in pieces[1:]:
        gain = gain * one(*cut)
    return gain


def centred(key, dims, scale, limit, shards=(), kind=jnp.bfloat16):
    drawn = jax.random.normal(key, dims, jnp.float32) * scale
    if len(shards) > 0:
        drawn = level_of(key, dims, shards, -0.22, 0.18) * drawn
    return jnp.clip(drawn, min=-limit, max=limit).astype(kind)


def setup_inputs(seed: int = 0) -> dict:
    streams_of = jax.random.split(jax.random.key(seed), 12)
    return {
        "queries": draw_queries(jax.random.fold_in(streams_of[11], 71), 0),
        "key_rows": draw_key_rows(jax.random.fold_in(streams_of[11], 71), 0),
        "values": centred(streams_of[2], (VTOKENS, VISION_WIDTH), 1.0, 6.0, ((0, 256),)),
        "segment_ids": draw_segment_ids(jax.random.fold_in(streams_of[11], 71), 0),
        "merger_norm_gain": jnp.clip(1.0 + 0.1 * jax.random.normal(streams_of[4], (VISION_WIDTH,), jnp.float32), 0.5, 1.5),
        "merge_weight": centred(streams_of[5], (MERGER_FEATURES, D), MERGER_FEATURES ** -0.5, 0.078125, ((0, 32), (1, 8))),
        "text_rows": centred(streams_of[6], (TOKENS, D), 1.0, 6.0, ((0, 256),)),
        "token_gain": jnp.clip(1.0 + 0.1 * jax.random.normal(streams_of[7], (D,), jnp.float32), 0.5, 1.5),
        "cotangent": centred(streams_of[8], (TOKENS, D), 1.0, 6.0, ((0, 256),)),
        "send_slot": draw_send_slot(jax.random.fold_in(streams_of[11], 71), 0),
        "place_pos": draw_place_pos(jax.random.fold_in(streams_of[11], 71), 0),
    }


EPS = 1e-06

def group_attention(queries, key_rows, values, segment_ids):
    length = VT_DEV * N_SEQ
    groups = queries.shape[0] // length

    def one_group(index):
        first = index.astype(jnp.int32) * length
        q_group = lax.dynamic_slice_in_dim(queries, first, length, 0).astype(jnp.float32).reshape(length, HEADS, HEAD_DIM)
        k_group = lax.dynamic_slice_in_dim(key_rows, first, length, 0).astype(jnp.float32).reshape(length, HEADS, HEAD_DIM)
        v_group = lax.dynamic_slice_in_dim(values, first, length, 0).astype(jnp.float32).reshape(length, HEADS, HEAD_DIM)
        images = lax.dynamic_slice_in_dim(segment_ids, first, length, 0)
        scores = jnp.einsum('qhd,khd->hqk', q_group, k_group) * HEAD_DIM ** (-0.5)
        same_image = images[:, None] == images[None, :]
        scores = jnp.where(same_image[None], scores, -1e+30)
        probs = jax.nn.softmax(scores, axis=-1)
        probs = lax.optimization_barrier(probs.astype(jnp.bfloat16)).astype(jnp.float32)
        output = jnp.einsum('hqk,khd->qhd', probs, v_group)
        return output.astype(jnp.bfloat16).reshape(length, VISION_WIDTH)
    return lax.map(one_group, jnp.arange(groups, dtype=jnp.int32)).reshape(-1, VISION_WIDTH)

def reference(queries, key_rows, values, segment_ids, merger_norm_gain, merge_weight, text_rows, token_gain, cotangent, send_slot, place_pos):
    attn = group_attention(queries, key_rows, values, segment_ids)
    patch_x = attn.astype(jnp.float32)
    mean_removed = patch_x - lax.optimization_barrier(jnp.mean(patch_x, axis=-1, keepdims=True))
    inverse_deviation = lax.rsqrt(lax.optimization_barrier(jnp.mean(mean_removed * mean_removed, axis=-1, keepdims=True)) + EPS)
    normalized_rows = mean_removed * inverse_deviation
    merged_patches = (normalized_rows * merger_norm_gain).astype(jnp.bfloat16).reshape(TOTAL_VIS_ROWS, MERGER_FEATURES)
    vision = jnp.dot(merged_patches, merge_weight, preferred_element_type=jnp.float32).astype(jnp.bfloat16)
    row_index = jnp.arange(TOTAL_VIS_ROWS, dtype=jnp.int32)
    device = row_index // DEVICE_VIS_ROWS
    group_index = device // N_SEQ
    seq_index = device % N_SEQ
    dest_device = send_slot // SLOT_ROWS * N_SEQ + seq_index
    arrival = dest_device * DEVICE_VIS_ROWS + group_index * SLOT_ROWS + send_slot % SLOT_ROWS
    target = (dest_device * TOK_DEV + place_pos[arrival]).astype(jnp.int32)
    inputs = text_rows.at[target].set(vision).astype(jnp.float32)
    inv_rms = lax.rsqrt(lax.optimization_barrier(jnp.mean(inputs * inputs, axis=-1, keepdims=True)) + EPS)
    hidden = (inputs * inv_rms * token_gain).astype(jnp.bfloat16)
    grad_y = cotangent.astype(jnp.float32) * token_gain
    input_grads = inv_rms * (grad_y - inputs * inv_rms * inv_rms * lax.optimization_barrier(jnp.mean(grad_y * inputs, axis=-1, keepdims=True)))
    back_rows = input_grads[target].astype(jnp.bfloat16)
    width = D // N_SEQ
    merged_gradient = jnp.zeros((TOTAL_VIS_ROWS, MERGER_FEATURES), jnp.float32)
    for column_block in range(N_SEQ):
        lower = column_block * width
        partial_term = jnp.dot(back_rows[:, lower:lower + width], merge_weight[:, lower:lower + width].T, preferred_element_type=jnp.float32)
        merged_gradient = merged_gradient + lax.optimization_barrier(partial_term.astype(jnp.bfloat16)).astype(jnp.float32)
    patch_gradient = merged_gradient.reshape(VTOKENS, VISION_WIDTH) * merger_norm_gain
    vision_output_gradient = inverse_deviation * (patch_gradient - lax.optimization_barrier(jnp.mean(patch_gradient, axis=-1, keepdims=True)) - normalized_rows * lax.optimization_barrier(jnp.mean(patch_gradient * normalized_rows, axis=-1, keepdims=True)))
    return (hidden, vision_output_gradient.astype(jnp.bfloat16))
```

```python
import functools

import jax
import jax.numpy as jnp
from jax import lax
from jax.experimental import pallas as pl
from jax.experimental.pallas import tpu as pltpu
from jax.sharding import PartitionSpec as P

VISION_WIDTH = 1280
HEAD_DIM = 80
MERGER_FEATURES = 5120
ROWS = 64
HALF = 640
EPS = 1e-06
NT = (((1,), (1,)), ((), ()))
F32 = jnp.float32
BF16 = jnp.bfloat16
LOG2E = 1.4426950408889634
VMEM = pl.BlockSpec(memory_space=pltpu.VMEM)
PARAMS = pltpu.CompilerParams(vmem_limit_bytes=48 * 2**20)


def iota(shape, axis):
    return lax.broadcasted_iota(jnp.int32, shape, axis)


def eye(n):
    return (iota((n, n), 0) == iota((n, n), 1)).astype(F32).astype(BF16)


def mm(a, b):
    return jnp.dot(a, b, preferred_element_type=F32)


def mm_nt(a, b):
    return lax.dot_general(a, b, NT, preferred_element_type=F32)


def onehot(mask):
    return mask.astype(F32).astype(BF16)


def block_of_granule(rho):
    g, half, i, p = rho // 16, rho // 8 % 2, rho // 4 % 2, rho % 4
    return (p * 2 + half) * 64 + g * 2 + i


def split_heads(q_ref, k_ref, v_ref, ids_ref, out_ref):
    one = eye(256)
    for t, ref in enumerate((q_ref, k_ref, v_ref)):
        for f in range(5):
            block = mm_nt(one, ref[:, 256 * f : 256 * f + 256]).astype(BF16)
            lower = 256 * f
            while lower < 256 * f + 256:
                dev = lower // 160
                upper = min(160 * (dev + 1), 256 * f + 256)
                out_ref[dev, 160 * t + lower - 160 * dev : 160 * t + upper - 160 * dev, :] = block[
                    lower - 256 * f : upper - 256 * f, :
                ]
                lower = upper
    ids = ids_ref[...]
    rows = jnp.where(iota((16, 256), 0) % 2 == 0, ids // 16, ids % 16)
    rows = rows.astype(F32).astype(BF16)
    for dev in range(8):
        out_ref[dev, 480:496, :] = rows


def attention(x_ref, o_ref, k_scr, idk_scr, s_scr):
    one = eye(256)
    scale = HEAD_DIM ** (-0.5) * LOG2E
    first, last, id_rows = [], [], []
    for j in range(8):
        for h in range(2):
            k_scr[j, h] = mm_nt(one, x_ref[j, 160 + 80 * h : 240 + 80 * h, :]).astype(BF16)
        parts = x_ref[j, 480:496, :]
        cols = mm_nt(one, parts)
        idk_scr[j] = jnp.broadcast_to(cols[:, 0:1] * 16.0 + cols[:, 1:2], (256, 128))
        parts = parts.astype(F32)
        row = parts[0:1] * 16.0 + parts[1:2]
        first.append(jnp.min(row))
        last.append(jnp.max(row))
    for i in range(8):
        parts = x_ref[i, 480:496, :].astype(F32)
        idq = parts[0:1] * 16.0 + parts[1:2]
        lo, hi = jnp.int32(0), jnp.int32(8)
        for j in range(8):
            if j < i:
                lo = lo + jnp.where(last[j] < first[i], 1, 0)
            if j > i:
                hi = hi - jnp.where(first[j] > last[i], 1, 0)

        def scores(j, m):
            idk = idk_scr[j]
            same = jnp.concatenate([idk, idk], axis=1) == idq
            new = []
            for h in range(2):
                s = mm(k_scr[j, h], x_ref[i, 80 * h : 80 * h + 80, :])
                s = jnp.where(same, s, -1e30)
                s_scr[h, j] = s
                new.append(jnp.maximum(m[h], jnp.max(s.reshape(32, 8, 256), axis=0)))
            return tuple(new)

        m = lax.fori_loop(lo, hi, scores, (jnp.full((8, 256), -1e30, F32),) * 2)
        top = [jnp.max(m[h], axis=0, keepdims=True) for h in range(2)]

        def weighted(j, carry):
            new = []
            for h in range(2):
                acc, total = carry[h]
                p = jnp.exp2((s_scr[h, j] - top[h]) * scale)
                total = total + jnp.sum(p.reshape(32, 8, 256), axis=0)
                acc = acc + mm(x_ref[j, 320 + 80 * h : 400 + 80 * h, :], p.astype(BF16))
                new.append((acc, total))
            return tuple(new)

        zero = (jnp.zeros((HEAD_DIM, 256), F32), jnp.zeros((8, 256), F32))
        done = lax.fori_loop(lo, hi, weighted, (zero, zero))
        for h in range(2):
            acc, total = done[h]
            total = jnp.sum(total, axis=0, keepdims=True)
            o_ref[i, 80 * h : 80 * h + 80, :] = (acc / total).astype(BF16)


def normalize(attn_t, one):
    x = jnp.concatenate([mm_nt(one, attn_t[256 * f : 256 * f + 256, :]) for f in range(5)], axis=1)
    x = x - jnp.mean(x, axis=1, keepdims=True)
    rstd = lax.rsqrt(jnp.mean(x * x, axis=1, keepdims=True) + EPS)
    return x * rstd, rstd


def merge(attn_ref, gain_ref, target_ref, out_ref):
    xhat, _ = normalize(attn_ref[...].reshape(VISION_WIDTH, 256), eye(256))
    merged = (xhat * gain_ref[...]).astype(BF16)
    stacked = jnp.concatenate([merged[:, :HALF], merged[:, HALF:]], axis=0)
    pick = onehot(iota((512, 512), 0) == target_ref[...])
    out_ref[...] = mm(pick, stacked).astype(BF16).reshape(32, 16, HALF)


def to_blocks(x_ref, out_ref):
    pick = onehot(iota((512, 512), 0) == block_of_granule(iota((512, 512), 1)))
    out_ref[...] = mm(pick, x_ref[...].reshape(512, HALF)).astype(BF16).reshape(8, ROWS, HALF)


def to_granules(x_ref, out_ref):
    pick = onehot(block_of_granule(iota((512, 512), 0)) == iota((512, 512), 1))
    out_ref[...] = mm(pick, x_ref[...].reshape(512, HALF)).astype(BF16).reshape(32, 16, HALF)


def project(a_ref, w_ref, out_ref):
    total = jnp.zeros((512, 256), F32)
    for b in range(8):
        total = total + mm(a_ref[:, b].reshape(512, HALF), w_ref[HALF * b : HALF * b + HALF, :])
    out_ref[...] = total.astype(BF16).reshape(8, ROWS, 256)


def project_back(a_ref, w_ref, out_ref):
    out_ref[...] = mm_nt(a_ref[...].reshape(512, 1024), w_ref[...]).astype(BF16).reshape(8, 1, ROWS, HALF)


def token_norm(vis_ref, text_ref, cot_ref, gain_ref, pos_ref, posc_ref, hid_ref, back_ref, inp_scr):
    place = onehot(iota((128, ROWS), 0) == pos_ref[...])
    pick = onehot(iota((ROWS, 128), 1) == posc_ref[...])
    taken = jnp.sum(place.astype(F32), axis=1, keepdims=True) > 0.5
    squares = jnp.zeros((128, 1), F32)
    products = jnp.zeros((128, 1), F32)
    for c in range(8):
        cols = slice(1024 * c, 1024 * c + 1024)
        inp = jnp.where(taken, mm(place, vis_ref[c]), text_ref[:, cols].astype(F32))
        inp_scr[:, cols] = inp
        squares = squares + jnp.sum(inp * inp, axis=1, keepdims=True)
        gy = cot_ref[:, cols].astype(F32) * gain_ref[:, cols]
        products = products + jnp.sum(gy * inp, axis=1, keepdims=True)
    r = lax.rsqrt(squares / 8192.0 + EPS)
    slope = r * r * (products / 8192.0)
    for c in range(8):
        cols = slice(1024 * c, 1024 * c + 1024)
        inp = inp_scr[:, cols]
        gain = gain_ref[:, cols]
        hid_ref[:, cols] = (inp * r * gain).astype(BF16)
        gy = cot_ref[:, cols].astype(F32) * gain
        grads = (r * (gy - inp * slope)).astype(BF16)
        back_ref[c] = mm(pick, grads).astype(BF16)


def patch_grads(attn_ref, g_ref, gain_ref, target_ref, out_ref):
    xhat, rstd = normalize(attn_ref[...].reshape(VISION_WIDTH, 256), eye(256))
    pick = onehot(iota((512, 512), 1) == target_ref[...])
    grads = mm(pick, g_ref[...].reshape(512, HALF))
    gy = jnp.concatenate([grads[:256], grads[256:]], axis=1) * gain_ref[...]
    mean = jnp.mean(gy, axis=1, keepdims=True)
    along = jnp.mean(gy * xhat, axis=1, keepdims=True)
    out_ref[...] = (rstd * (gy - mean - xhat * along)).astype(BF16)


def local(kernel, shape, dtype, n_in, scratch=(), name=None):
    many = isinstance(shape, list)
    out = [jax.ShapeDtypeStruct(s, dtype) for s in shape] if many else jax.ShapeDtypeStruct(shape, dtype)
    return pl.pallas_call(
        kernel,
        out_shape=out,
        in_specs=[VMEM] * n_in,
        out_specs=[VMEM] * len(shape) if many else VMEM,
        scratch_shapes=list(scratch),
        compiler_params=PARAMS,
        name=name,
    )


def body(
    queries,
    key_rows,
    values,
    segment_ids,
    merger_norm_gain,
    merge_weight,
    text_rows,
    token_gain,
    cotangent,
    send_slot,
    place_pos,
):
    w = lax.all_gather(merge_weight, "grp", axis=0, tiled=True)
    gain = merger_norm_gain.reshape(1, VISION_WIDTH)
    slot = jnp.tile(jnp.repeat(send_slot, 4), 2)
    kappa = jnp.arange(512, dtype=jnp.int32)
    target = slot // 2 * 16 + kappa // 256 * 8 + slot % 2 * 4 + kappa % 4

    x = local(split_heads, (8, 496, 256), BF16, 4, name="split_heads")(
        queries, key_rows, values, segment_ids.reshape(1, 256)
    )
    x = lax.all_to_all(x, "seq", split_axis=0, concat_axis=0, tiled=True)
    o = local(
        attention,
        (8, 160, 256),
        BF16,
        1,
        [
            pltpu.VMEM((8, 2, 256, HEAD_DIM), BF16),
            pltpu.VMEM((8, 256, 128), F32),
            pltpu.VMEM((2, 8, 256, 256), F32),
        ],
        name="attention",
    )(x)
    attn = lax.all_to_all(o, "seq", split_axis=0, concat_axis=0, tiled=True)
    routed = local(merge, (32, 16, HALF), BF16, 3, name="merge")(attn, gain, target.reshape(1, 512))
    routed = lax.all_to_all(routed, "grp", split_axis=0, concat_axis=0, tiled=True)
    blocks = local(to_blocks, (8, ROWS, HALF), BF16, 1, name="to_blocks")(routed)
    gathered = lax.all_gather(blocks, "seq", axis=0)
    vision = pl.pallas_call(
        project,
        grid=(4,),
        out_shape=jax.ShapeDtypeStruct((8, ROWS, 1024), BF16),
        in_specs=[
            pl.BlockSpec((8, 8, ROWS, HALF), lambda n: (0, 0, 0, 0)),
            pl.BlockSpec((MERGER_FEATURES, 256), lambda n: (0, n)),
        ],
        out_specs=pl.BlockSpec((8, ROWS, 256), lambda n: (0, 0, n)),
        compiler_params=PARAMS,
        name="project",
    )(gathered, w)
    vision = lax.all_to_all(vision, "seq", split_axis=0, concat_axis=0, tiled=True)
    hidden, back = local(
        token_norm, [(128, 8192), (8, ROWS, 1024)], BF16, 6, [pltpu.VMEM((128, 8192), F32)], name="token_norm"
    )(
        vision,
        text_rows,
        cotangent,
        token_gain.reshape(1, 8192),
        place_pos.reshape(1, ROWS),
        place_pos.reshape(ROWS, 1),
    )
    back = lax.all_to_all(back, "seq", split_axis=0, concat_axis=0, tiled=True)
    terms = pl.pallas_call(
        project_back,
        grid=(8,),
        out_shape=jax.ShapeDtypeStruct((8, 8, ROWS, HALF), BF16),
        in_specs=[
            pl.BlockSpec((8, ROWS, 1024), lambda n: (0, 0, 0)),
            pl.BlockSpec((HALF, 1024), lambda n: (n, 0)),
        ],
        out_specs=pl.BlockSpec((8, 1, ROWS, HALF), lambda n: (0, n, 0, 0)),
        compiler_params=PARAMS,
        name="project_back",
    )(back, w)
    summed = lax.psum_scatter(terms.reshape(8 * 512, HALF), "seq", scatter_dimension=0, tiled=True)
    granules = local(to_granules, (32, 16, HALF), BF16, 1, name="to_granules")(summed.reshape(8, ROWS, HALF))
    granules = lax.all_to_all(granules, "grp", split_axis=0, concat_axis=0, tiled=True)
    vision_output_gradient = local(patch_grads, (256, VISION_WIDTH), BF16, 4, name="patch_grads")(
        attn, granules, gain, target.reshape(512, 1)
    )
    return hidden, vision_output_gradient


def solution(mesh):
    in_specs = (
        P(("grp", "seq"), None),
        P(("grp", "seq"), None),
        P(("grp", "seq"), None),
        P(("grp", "seq")),
        P(),
        P("grp", "seq"),
        P(("grp", "seq"), None),
        P(),
        P(("grp", "seq"), None),
        P(("grp", "seq")),
        P(("grp", "seq")),
    )
    out_specs = (P(("grp", "seq"), None), P(("grp", "seq"), None))
    return jax.shard_map(body, mesh=mesh, in_specs=in_specs, out_specs=out_specs, check_vma=False)
```

```python
import jax
import jax.numpy as jnp
from jax import lax
from jax.experimental import pallas as pl
from jax.experimental.pallas import tpu as pltpu
from jax.sharding import PartitionSpec as P

VISION_WIDTH = 1280
HEAD_DIM = 80
MERGER_FEATURES = 5120
ROWS = 64
HALF = 640
EPS = 1e-06
NT = (((1,), (1,)), ((), ()))
F32 = jnp.float32
BF16 = jnp.bfloat16
LOG2E = 1.4426950408889634
MESH = pl.DeviceIdType.MESH
DMA = pltpu.SemaphoreType.DMA
ANY = pl.BlockSpec(memory_space=pl.ANY)
VMEM = pl.BlockSpec(memory_space=pltpu.VMEM)


def iota(shape, axis):
    return lax.broadcasted_iota(jnp.int32, shape, axis)


def eye(n):
    return (iota((n, n), 0) == iota((n, n), 1)).astype(F32).astype(BF16)


def mm(a, b):
    return jnp.dot(a, b, preferred_element_type=F32)


def mm_nt(a, b):
    return lax.dot_general(a, b, NT, preferred_element_type=F32)


def onehot(mask):
    return mask.astype(F32).astype(BF16)


def block_of_granule(rho):
    g, half, i, p = rho // 16, rho // 8 % 2, rho // 4 % 2, rho % 4
    return (p * 2 + half) * 64 + g * 2 + i


def attention(x_ref, o_ref, k_scr, idk_scr, s_scr):
    one = eye(256)
    scale = HEAD_DIM ** (-0.5) * LOG2E
    first, last, id_rows = [], [], []
    for j in range(8):
        for h in range(2):
            k_scr[j, h] = mm_nt(one, x_ref[j, 160 + 80 * h : 240 + 80 * h, :]).astype(BF16)
        parts = x_ref[j, 480:496, :]
        cols = mm_nt(one, parts)
        idk_scr[j] = jnp.broadcast_to(cols[:, 0:1] * 16.0 + cols[:, 1:2], (256, 128))
        parts = parts.astype(F32)
        row = parts[0:1] * 16.0 + parts[1:2]
        first.append(jnp.min(row))
        last.append(jnp.max(row))
    for i in range(8):
        parts = x_ref[i, 480:496, :].astype(F32)
        idq = parts[0:1] * 16.0 + parts[1:2]
        lo, hi = jnp.int32(0), jnp.int32(8)
        for j in range(8):
            if j < i:
                lo = lo + jnp.where(last[j] < first[i], 1, 0)
            if j > i:
                hi = hi - jnp.where(first[j] > last[i], 1, 0)

        def scores(j, m):
            idk = idk_scr[j]
            same = jnp.concatenate([idk, idk], axis=1) == idq
            new = []
            for h in range(2):
                s = mm(k_scr[j, h], x_ref[i, 80 * h : 80 * h + 80, :])
                s = jnp.where(same, s, -1e30)
                s_scr[h, j] = s
                new.append(jnp.maximum(m[h], jnp.max(s.reshape(32, 8, 256), axis=0)))
            return tuple(new)

        m = lax.fori_loop(lo, hi, scores, (jnp.full((8, 256), -1e30, F32),) * 2)
        top = [jnp.max(m[h], axis=0, keepdims=True) for h in range(2)]

        def weighted(j, carry):
            new = []
            for h in range(2):
                acc, total = carry[h]
                p = jnp.exp2((s_scr[h, j] - top[h]) * scale)
                total = total + jnp.sum(p.reshape(32, 8, 256), axis=0)
                acc = acc + mm(x_ref[j, 320 + 80 * h : 400 + 80 * h, :], p.astype(BF16))
                new.append((acc, total))
            return tuple(new)

        zero = (jnp.zeros((HEAD_DIM, 256), F32), jnp.zeros((8, 256), F32))
        done = lax.fori_loop(lo, hi, weighted, (zero, zero))
        for h in range(2):
            acc, total = done[h]
            total = jnp.sum(total, axis=0, keepdims=True)
            o_ref[i, 80 * h : 80 * h + 80, :] = (acc / total).astype(BF16)


def normalize(attn_t, one):
    x = jnp.concatenate([mm_nt(one, attn_t[256 * f : 256 * f + 256, :]) for f in range(5)], axis=1)
    x = x - jnp.mean(x, axis=1, keepdims=True)
    rstd = lax.rsqrt(jnp.mean(x * x, axis=1, keepdims=True) + EPS)
    return x * rstd, rstd


def greet(devices):
    barrier = pltpu.get_barrier_semaphore()
    for device in devices:
        pl.semaphore_signal(barrier, inc=1, device_id=device, device_id_type=MESH)
    pl.semaphore_wait(barrier, len(devices))


def remote(src, dst, send_sem, recv_sem, device):
    return pltpu.make_async_remote_copy(
        src_ref=src, dst_ref=dst, send_sem=send_sem, recv_sem=recv_sem, device_id=device, device_id_type=MESH
    )


def others(axis, n):
    me = lax.axis_index(axis)
    return [{axis: lax.rem(me + k, n)} for k in range(1, n)]


def exchange(axis, n, src, dst, send_sem, recv_sem, local_sem):
    me = lax.axis_index(axis)
    copies = []
    for k in range(1, n):
        d = lax.rem(me + k, n)
        copy = remote(src.at[d], dst.at[me], send_sem.at[k], recv_sem.at[k], {axis: d})
        copy.start()
        copies.append(copy)
    own = pltpu.make_async_copy(src.at[me], dst.at[me], local_sem)
    own.start()
    return copies + [own]


def finish(copies):
    for copy in copies:
        copy.wait()


def heads_out(q_ref, k_ref, v_ref, ids_ref, out_ref, parts, send_sem, recv_sem, local_sem):
    one = eye(256)
    for t, ref in enumerate((q_ref, k_ref, v_ref)):
        for f in range(5):
            block = mm_nt(one, ref[:, 256 * f : 256 * f + 256]).astype(BF16)
            lower = 256 * f
            while lower < 256 * f + 256:
                dev = lower // 160
                upper = min(160 * (dev + 1), 256 * f + 256)
                parts[dev, 160 * t + lower - 160 * dev : 160 * t + upper - 160 * dev, :] = block[
                    lower - 256 * f : upper - 256 * f, :
                ]
                lower = upper
    ids = ids_ref[...]
    rows = jnp.where(iota((16, 256), 0) % 2 == 0, ids // 16, ids % 16)
    rows = rows.astype(F32).astype(BF16)
    for dev in range(8):
        parts[dev, 480:496, :] = rows
    greet(others("seq", 8))
    finish(exchange("seq", 8, parts, out_ref, send_sem, recv_sem, local_sem))


def neighbours():
    me = lax.axis_index("seq")
    x, core = me // 2, lax.rem(me, 2)
    chip = lambda k: lax.rem(x + k, 4) * 2 + core
    return me, chip(1), chip(3), chip(2), x * 2 + 1 - core


def merge_and_gather(
    o_ref, gain_ref, target_ref, attn_ref, a_ref, granules, routed, s1, r1, s2, r2, l_sem, s3, r3
):
    greet(others("seq", 8) + others("grp", 32))
    finish(exchange("seq", 8, o_ref, attn_ref, s1, r1, l_sem))
    xhat, _ = normalize(attn_ref[...].reshape(VISION_WIDTH, 256), eye(256))
    merged = (xhat * gain_ref[...]).astype(BF16)
    stacked = jnp.concatenate([merged[:, :HALF], merged[:, HALF:]], axis=0)
    pick = onehot(iota((512, 512), 0) == target_ref[...])
    granules[...] = mm(pick, stacked).astype(BF16).reshape(32, 16, HALF)
    finish(exchange("grp", 32, granules, routed, s2, r2, l_sem))
    me, right, left, across, twin = neighbours()
    pick = onehot(iota((512, 512), 0) == block_of_granule(iota((512, 512), 1)))
    mine = mm(pick, routed[...].reshape(512, HALF)).astype(BF16)
    for b in range(8):
        a_ref[b, me] = mine[64 * b : 64 * b + 64]
    upper, lower = pl.ds(0, 32), pl.ds(32, 32)

    def piece(kind, b, owner, rows, device):
        place = a_ref.at[b, owner] if rows is None else a_ref.at[b, owner, rows]
        return remote(place, place, s3.at[kind, b], r3.at[kind, b], {"seq": device})

    def own(kind, b):
        return piece(kind, b, me, None, (right, left, twin)[kind])

    def forward(kind, b):
        if kind == 3:
            return piece(3, b, left, upper, right)
        return piece(4, b, right, lower, left)

    def to_twin(kind, b):
        owner = (left, right, across, across)[kind - 5]
        return piece(kind, b, owner, (None, None, upper, lower)[kind - 5], twin)

    def first(b, _):
        for kind in range(3):
            own(kind, b).start()
        return 0

    def second(b, _):
        own(0, b).wait_recv()
        forward(3, b).start()
        to_twin(5, b).start()
        own(1, b).wait_recv()
        forward(4, b).start()
        to_twin(6, b).start()
        return 0

    def third(b, _):
        forward(3, b).wait_recv()
        to_twin(7, b).start()
        forward(4, b).wait_recv()
        to_twin(8, b).start()
        return 0

    def last(b, _):
        own(0, b).wait_send()
        own(1, b).wait_send()
        own(2, b).wait()
        forward(3, b).wait_send()
        forward(4, b).wait_send()
        for kind in range(5, 9):
            to_twin(kind, b).wait()
        return 0

    for step in (first, second, third, last):
        lax.fori_loop(0, 8, step, 0)


def language(
    a_ref, w_ref, text_ref, cot_ref, gain_ref, pos_ref, posc_ref, attn_ref, mgain_ref, target_ref,
    hid_ref, out_ref,
    w, text, cot, proj, vis, inp_scr, back, ret, terms, twin_terms, far, near, summed, granules, arrived,
    w_sem, t_sem, s1, r1, s2, r2, s3, r3, s4, r4, l_sem,
):
    loads = [pltpu.make_async_copy(w_ref.at[:, pl.ds(256 * n, 256)], w.at[n], w_sem.at[n]) for n in range(4)]
    loads += [pltpu.make_async_copy(text_ref, text, t_sem.at[0]), pltpu.make_async_copy(cot_ref, cot, t_sem.at[1])]
    for load in loads:
        load.start()
    greet(others("seq", 8) + others("grp", 32))
    me, right, left, across, twin = neighbours()

    def vision_tile(n, k):
        d = lax.rem(me + k, 8)
        return remote(proj.at[n, d], vis.at[n, me], s1.at[n, k], r1.at[n, k], {"seq": d})

    def project(n, _):
        pltpu.make_async_copy(w_ref.at[:, pl.ds(0, 256)], w.at[n], w_sem.at[n]).wait()
        total = jnp.zeros((512, 256), F32)
        for b in range(8):
            total = total + mm(a_ref[b].reshape(512, HALF), w[n, HALF * b : HALF * b + HALF, :])
        proj[n] = total.astype(BF16).reshape(8, ROWS, 256)
        for k in range(1, 8):
            vision_tile(n, k).start()
        vis[n, me] = proj[n, me]
        return 0

    lax.fori_loop(0, 4, project, 0)
    loads[4].wait()
    loads[5].wait()

    place = onehot(iota((128, ROWS), 0) == pos_ref[...])
    pick = onehot(iota((ROWS, 128), 1) == posc_ref[...])
    taken = jnp.sum(place.astype(F32), axis=1, keepdims=True) > 0.5

    def place_tile(n, carry):
        for k in range(1, 8):
            vision_tile(n, k).wait_recv()

        def block(c, carry):
            squares, products = carry
            cols = pl.ds(pl.multiple_of(c * 1024 + n * 256, 256), 256)
            inp = jnp.where(taken, mm(place, vis[n, c]), text[:, cols].astype(F32))
            inp_scr[:, cols] = inp
            gy = cot[:, cols].astype(F32) * gain_ref[:, cols]
            return squares + inp * inp, products + gy * inp

        return lax.fori_loop(0, 8, block, carry)

    zero = jnp.zeros((128, 256), F32)
    squares, products = lax.fori_loop(0, 4, place_tile, (zero, zero))
    squares = jnp.sum(squares, axis=1, keepdims=True)
    products = jnp.sum(products, axis=1, keepdims=True)
    r = lax.rsqrt(squares / 8192.0 + EPS)
    slope = r * r * (products / 8192.0)

    def back_copy(k):
        d = lax.rem(me + k, 8)
        return remote(back.at[d], ret.at[me], s2.at[k], r2.at[k], {"seq": d})

    def grads(k, _):
        c = lax.rem(me + k, 8)
        cols = pl.ds(pl.multiple_of(c * 1024, 1024), 1024)
        gy = cot[:, cols].astype(F32) * gain_ref[:, cols]
        grad = (r * (gy - inp_scr[:, cols] * slope)).astype(BF16)
        back[c] = mm(pick, grad).astype(BF16)
        back_copy(k).start()
        return 0

    lax.fori_loop(1, 8, grads, 0)
    cols = pl.ds(pl.multiple_of(me * 1024, 1024), 1024)
    gy = cot[:, cols].astype(F32) * gain_ref[:, cols]
    grad = (r * (gy - inp_scr[:, cols] * slope)).astype(BF16)
    ret[me] = mm(pick, grad).astype(BF16)

    def hidden(c, _):
        cols = pl.ds(pl.multiple_of(c * 1024, 1024), 1024)
        hid_ref[:, cols] = (inp_scr[:, cols] * r * gain_ref[:, cols]).astype(BF16)
        return 0

    lax.fori_loop(0, 8, hidden, 0)
    for k in range(1, 8):
        back_copy(k).wait_recv()

    core = lax.rem(me, 2)
    x = me // 2
    chip_right, chip_left, chip_across = lax.rem(x + 1, 4), lax.rem(x + 3, 4), lax.rem(x + 2, 4)
    upper, lower = pl.ds(0, 32), pl.ds(32, 32)

    def to_twin(b):
        return remote(terms.at[b, 1 - core], twin_terms.at[b], s3.at[0, b], r3.at[0, b], {"seq": twin})

    def far_right(b):
        return remote(terms.at[b, core, chip_across, upper], far.at[b, upper], s3.at[1, b], r3.at[1, b], {"seq": right})

    def far_left(b):
        return remote(terms.at[b, core, chip_across, lower], far.at[b, lower], s3.at[2, b], r3.at[2, b], {"seq": left})

    def near_right(b):
        return remote(terms.at[b, core, chip_right], near.at[b, 0], s3.at[3, b], r3.at[3, b], {"seq": right})

    def near_left(b):
        return remote(terms.at[b, core, chip_left], near.at[b, 1], s3.at[4, b], r3.at[4, b], {"seq": left})

    def step(i, _):
        @pl.when(i < 8)
        def _():
            b = i
            rows = pl.ds(pl.multiple_of(b * HALF, HALF), HALF)
            total = jnp.zeros((512, HALF), F32)
            for n in range(4):
                total = total + mm_nt(ret[:, :, 256 * n : 256 * n + 256].reshape(512, 256), w[n, rows, :])
            total = total.astype(BF16)
            for s in range(8):
                terms[b, s % 2, s // 2] = total[64 * s : 64 * s + 64]
            to_twin(b).start()

        @pl.when((i >= 1) & (i < 9))
        def _():
            b = i - 1
            to_twin(b).wait_recv()
            both = terms[b, core].astype(F32) + twin_terms[b].astype(F32)
            terms[b, core] = both.astype(BF16)
            far_right(b).start()
            far_left(b).start()

        @pl.when((i >= 2) & (i < 10))
        def _():
            b = i - 2
            far_right(b).wait_recv()
            terms[b, core, chip_right, upper] = (
                terms[b, core, chip_right, upper].astype(F32) + far[b, upper].astype(F32)
            ).astype(BF16)
            near_right(b).start()
            far_left(b).wait_recv()
            terms[b, core, chip_left, lower] = (
                terms[b, core, chip_left, lower].astype(F32) + far[b, lower].astype(F32)
            ).astype(BF16)
            near_left(b).start()

        @pl.when(i >= 3)
        def _():
            b = i - 3
            near_right(b).wait_recv()
            near_left(b).wait_recv()
            total = terms[b, core, x].astype(F32) + near[b, 0].astype(F32) + near[b, 1].astype(F32)
            summed[b] = total.astype(BF16)

        return 0

    lax.fori_loop(0, 11, step, 0)
    pick = onehot(block_of_granule(iota((512, 512), 0)) == iota((512, 512), 1))
    granules[...] = mm(pick, summed[...].reshape(512, HALF)).astype(BF16).reshape(32, 16, HALF)
    copies = exchange("grp", 32, granules, arrived, s4, r4, l_sem)

    def settle(b, _):
        for copy in (to_twin(b), far_right(b), far_left(b), near_right(b), near_left(b)):
            copy.wait_send()
        return 0

    lax.fori_loop(0, 8, settle, 0)
    for n in range(4):
        for k in range(1, 8):
            vision_tile(n, k).wait_send()
    for k in range(1, 8):
        back_copy(k).wait_send()
    xhat, rstd = normalize(attn_ref[...].reshape(VISION_WIDTH, 256), eye(256))
    pick = onehot(iota((512, 512), 1) == target_ref[...])
    finish(copies)
    grads = mm(pick, arrived[...].reshape(512, HALF))
    gy = jnp.concatenate([grads[:256], grads[256:]], axis=1) * mgain_ref[...]
    mean = jnp.mean(gy, axis=1, keepdims=True)
    along = jnp.mean(gy * xhat, axis=1, keepdims=True)
    out_ref[...] = (rstd * (gy - mean - xhat * along)).astype(BF16)


def params(collective_id=None):
    if collective_id is None:
        return pltpu.CompilerParams(vmem_limit_bytes=48 * 2**20)
    return pltpu.CompilerParams(
        vmem_limit_bytes=58 * 2**20, collective_id=collective_id, has_side_effects=True
    )


def shaped(*shape, dtype=BF16):
    return jax.ShapeDtypeStruct(shape, dtype)


def body(
    queries,
    key_rows,
    values,
    segment_ids,
    merger_norm_gain,
    merge_weight,
    text_rows,
    token_gain,
    cotangent,
    send_slot,
    place_pos,
):
    w = lax.all_gather(merge_weight, "grp", axis=0, tiled=True)
    gain = merger_norm_gain.reshape(1, VISION_WIDTH)
    slot = jnp.tile(jnp.repeat(send_slot, 4), 2)
    kappa = jnp.arange(512, dtype=jnp.int32)
    target = slot // 2 * 16 + kappa // 256 * 8 + slot % 2 * 4 + kappa % 4

    x = pl.pallas_call(
        heads_out,
        out_shape=shaped(8, 496, 256),
        in_specs=[VMEM] * 4,
        out_specs=VMEM,
        scratch_shapes=[pltpu.VMEM((8, 496, 256), BF16), DMA((8,)), DMA((8,)), DMA(())],
        compiler_params=params(1),
        name="heads_out",
    )(queries, key_rows, values, segment_ids.reshape(1, 256))
    o = pl.pallas_call(
        attention,
        out_shape=shaped(8, 160, 256),
        in_specs=[VMEM],
        out_specs=VMEM,
        scratch_shapes=[
            pltpu.VMEM((8, 2, 256, HEAD_DIM), BF16),
            pltpu.VMEM((8, 256, 128), F32),
            pltpu.VMEM((2, 8, 256, 256), F32),
        ],
        compiler_params=params(),
        name="attention",
    )(x)
    attn, a = pl.pallas_call(
        merge_and_gather,
        out_shape=[shaped(8, 160, 256), shaped(8, 8, ROWS, HALF)],
        in_specs=[VMEM] * 3,
        out_specs=[VMEM] * 2,
        scratch_shapes=[
            pltpu.VMEM((32, 16, HALF), BF16),
            pltpu.VMEM((32, 16, HALF), BF16),
            DMA((8,)),
            DMA((8,)),
            DMA((32,)),
            DMA((32,)),
            DMA(()),
            DMA((9, 8)),
            DMA((9, 8)),
        ],
        compiler_params=params(2),
        name="merge_and_gather",
    )(o, gain, target.reshape(1, 512))
    return pl.pallas_call(
        language,
        out_shape=[shaped(128, 8192), shaped(256, VISION_WIDTH)],
        in_specs=[VMEM, ANY, ANY, ANY] + [VMEM] * 6,
        out_specs=[VMEM] * 2,
        scratch_shapes=[
            pltpu.VMEM((4, MERGER_FEATURES, 256), BF16),
            pltpu.VMEM((128, 8192), BF16),
            pltpu.VMEM((128, 8192), BF16),
            pltpu.VMEM((4, 8, ROWS, 256), BF16),
            pltpu.VMEM((4, 8, ROWS, 256), BF16),
            pltpu.VMEM((128, 8192), F32),
            pltpu.VMEM((8, ROWS, 1024), BF16),
            pltpu.VMEM((8, ROWS, 1024), BF16),
            pltpu.VMEM((8, 2, 4, ROWS, HALF), BF16),
            pltpu.VMEM((8, 4, ROWS, HALF), BF16),
            pltpu.VMEM((8, ROWS, HALF), BF16),
            pltpu.VMEM((8, 2, ROWS, HALF), BF16),
            pltpu.VMEM((8, ROWS, HALF), BF16),
            pltpu.VMEM((32, 16, HALF), BF16),
            pltpu.VMEM((32, 16, HALF), BF16),
            DMA((4,)),
            DMA((2,)),
            DMA((4, 8)),
            DMA((4, 8)),
            DMA((8,)),
            DMA((8,)),
            DMA((5, 8)),
            DMA((5, 8)),
            DMA((32,)),
            DMA((32,)),
            DMA(()),
        ],
        compiler_params=params(3),
        name="language",
    )(
        a,
        w,
        text_rows,
        cotangent,
        token_gain.reshape(1, 8192),
        place_pos.reshape(1, ROWS),
        place_pos.reshape(ROWS, 1),
        attn,
        gain,
        target.reshape(512, 1),
    )


def solution(mesh):
    in_specs = (
        P(("grp", "seq"), None),
        P(("grp", "seq"), None),
        P(("grp", "seq"), None),
        P(("grp", "seq")),
        P(),
        P("grp", "seq"),
        P(("grp", "seq"), None),
        P(),
        P(("grp", "seq"), None),
        P(("grp", "seq")),
        P(("grp", "seq")),
    )
    out_specs = (P(("grp", "seq"), None), P(("grp", "seq"), None))
    return jax.shard_map(body, mesh=mesh, in_specs=in_specs, out_specs=out_specs, check_vma=False)
```

```python
import jax
import jax.numpy as jnp
from jax import lax
from jax.experimental import pallas as pl
from jax.experimental.pallas import tpu as pltpu
from jax.sharding import PartitionSpec as P

VISION_WIDTH = 1280
HEAD_DIM = 80
MERGER_FEATURES = 5120
ROWS = 64
PART = 32
HALF = 640
EPS = 1e-06
NT = (((1,), (1,)), ((), ()))
F32 = jnp.float32
BF16 = jnp.bfloat16
LOG2E = 1.4426950408889634
MESH = pl.DeviceIdType.MESH
DMA = pltpu.SemaphoreType.DMA
ANY = pl.BlockSpec(memory_space=pl.ANY)
VMEM = pl.BlockSpec(memory_space=pltpu.VMEM)


def iota(shape, axis):
    return lax.broadcasted_iota(jnp.int32, shape, axis)


def eye(n):
    return (iota((n, n), 0) == iota((n, n), 1)).astype(F32).astype(BF16)


def mm(a, b):
    return jnp.dot(a, b, preferred_element_type=F32)


def mm_nt(a, b):
    return lax.dot_general(a, b, NT, preferred_element_type=F32)


def onehot(mask):
    return mask.astype(F32).astype(BF16)


def block_of_granule(rho):
    kk, half, i, p = rho // 16, rho // 8 % 2, rho // 4 % 2, rho % 4
    return (p * 2 + half) * PART + kk * 2 + i


def attention(x_ref, o_ref, k_scr, idk_scr, s_scr):
    one = eye(256)
    scale = HEAD_DIM ** (-0.5) * LOG2E
    first, last, id_rows = [], [], []
    for j in range(8):
        for h in range(2):
            k_scr[j, h] = mm_nt(one, x_ref[j, 160 + 80 * h : 240 + 80 * h, :]).astype(BF16)
        parts = x_ref[j, 480:496, :]
        cols = mm_nt(one, parts)
        idk_scr[j] = jnp.broadcast_to(cols[:, 0:1] * 16.0 + cols[:, 1:2], (256, 128))
        parts = parts.astype(F32)
        row = parts[0:1] * 16.0 + parts[1:2]
        first.append(jnp.min(row))
        last.append(jnp.max(row))
    for i in range(8):
        parts = x_ref[i, 480:496, :].astype(F32)
        idq = parts[0:1] * 16.0 + parts[1:2]
        lo, hi = jnp.int32(0), jnp.int32(8)
        for j in range(8):
            if j < i:
                lo = lo + jnp.where(last[j] < first[i], 1, 0)
            if j > i:
                hi = hi - jnp.where(first[j] > last[i], 1, 0)

        def scores(j, m):
            idk = idk_scr[j]
            same = jnp.concatenate([idk, idk], axis=1) == idq
            new = []
            for h in range(2):
                s = mm(k_scr[j, h], x_ref[i, 80 * h : 80 * h + 80, :])
                s = jnp.where(same, s, -1e30)
                s_scr[h, j] = s
                new.append(jnp.maximum(m[h], jnp.max(s.reshape(32, 8, 256), axis=0)))
            return tuple(new)

        m = lax.fori_loop(lo, hi, scores, (jnp.full((8, 256), -1e30, F32),) * 2)
        top = [jnp.max(m[h], axis=0, keepdims=True) for h in range(2)]

        def weighted(j, carry):
            new = []
            for h in range(2):
                acc, total = carry[h]
                p = jnp.exp2((s_scr[h, j] - top[h]) * scale)
                total = total + jnp.sum(p.reshape(32, 8, 256), axis=0)
                acc = acc + mm(x_ref[j, 320 + 80 * h : 400 + 80 * h, :], p.astype(BF16))
                new.append((acc, total))
            return tuple(new)

        zero = (jnp.zeros((HEAD_DIM, 256), F32), jnp.zeros((8, 256), F32))
        done = lax.fori_loop(lo, hi, weighted, (zero, zero))
        for h in range(2):
            acc, total = done[h]
            total = jnp.sum(total, axis=0, keepdims=True)
            o_ref[i, 80 * h : 80 * h + 80, :] = (acc / total).astype(BF16)


def normalize(attn_t, one):
    x = jnp.concatenate([mm_nt(one, attn_t[256 * f : 256 * f + 256, :]) for f in range(5)], axis=1)
    x = x - jnp.mean(x, axis=1, keepdims=True)
    rstd = lax.rsqrt(jnp.mean(x * x, axis=1, keepdims=True) + EPS)
    return x * rstd, rstd


def greet(devices):
    barrier = pltpu.get_barrier_semaphore()
    for device in devices:
        pl.semaphore_signal(barrier, inc=1, device_id=device, device_id_type=MESH)
    pl.semaphore_wait(barrier, len(devices))


def remote(src, dst, send_sem, recv_sem, device):
    return pltpu.make_async_remote_copy(
        src_ref=src, dst_ref=dst, send_sem=send_sem, recv_sem=recv_sem, device_id=device, device_id_type=MESH
    )


def others(axis, n):
    me = lax.axis_index(axis)
    return [{axis: lax.rem(me + k, n)} for k in range(1, n)]


def exchange(src, dst, send_sem, recv_sem, local_sem):
    me = lax.axis_index("seq")
    copies = []
    for k in range(1, 8):
        d = lax.rem(me + k, 8)
        copy = remote(src.at[d], dst.at[me], send_sem.at[k], recv_sem.at[k], {"seq": d})
        copy.start()
        copies.append(copy)
    own = pltpu.make_async_copy(src.at[me], dst.at[me], local_sem)
    own.start()
    return copies + [own]


def finish(copies):
    for copy in copies:
        copy.wait()


def heads_out(
    q_ref, k_ref, v_ref, ids_ref, out_ref, parts, send_sem, recv_sem, local_sem
):
    one = eye(256)
    greet(others("seq", 8))
    ids = ids_ref[...]
    rows = jnp.where(iota((16, 256), 0) % 2 == 0, ids // 16, ids % 16)
    rows = rows.astype(F32).astype(BF16)
    for dev in range(8):
        parts[dev, 480:496, :] = rows
    for t, ref in enumerate((q_ref, k_ref, v_ref)):
        for f in range(5):
            block = mm_nt(one, ref[:, 256 * f : 256 * f + 256]).astype(BF16)
            lower = 256 * f
            while lower < 256 * f + 256:
                dev = lower // 160
                upper = min(160 * (dev + 1), 256 * f + 256)
                parts[dev, 160 * t + lower - 160 * dev : 160 * t + upper - 160 * dev, :] = block[
                    lower - 256 * f : upper - 256 * f, :
                ]
                lower = upper
    finish(exchange(parts, out_ref, send_sem, recv_sem, local_sem))


def neighbours():
    me = lax.axis_index("seq")
    x, core = me // 2, lax.rem(me, 2)
    chip = lambda k: lax.rem(x + k, 4) * 2 + core
    return me, chip(1), chip(3), chip(2), x * 2 + 1 - core


def granule_of_patch(slot_ref):
    slot = jnp.broadcast_to(slot_ref[...], (8, ROWS)).astype(F32).astype(BF16)
    repeat = onehot(iota((ROWS, 512), 0) == iota((ROWS, 512), 1) % 256 // 4)
    slot = mm(slot, repeat)[0:1].astype(jnp.int32)
    kappa = iota((1, 512), 1)
    target = slot // 2 * 16 + kappa // 256 * 8 + slot % 2 * 4 + kappa % 4
    return onehot(iota((512, 512), 0) == target)


def merge_and_gather(
    o_ref, gain_ref, slot_ref, attn_ref, a_ref, granules, routed, s1, r1, s2, r2, l_sem, s3, r3
):
    greet(others("seq", 8) + others("grp", 32))
    copies = exchange(o_ref, attn_ref, s1, r1, l_sem)
    g = lax.axis_index("grp")
    move = granule_of_patch(slot_ref)
    to_block = onehot(iota((256, 256), 0) == block_of_granule(iota((256, 256), 1)))
    finish(copies)
    xhat, _ = normalize(attn_ref[...].reshape(VISION_WIDTH, 256), eye(256))
    merged = (xhat * gain_ref[...]).astype(BF16)
    stacked = jnp.concatenate([merged[:, :HALF], merged[:, HALF:]], axis=0)
    granules[...] = mm(move, stacked).astype(BF16).reshape(32, 16, HALF)

    own = pltpu.make_async_copy(granules.at[g], routed.at[0, 0], l_sem)
    own.start()
    routes = [{}, {}]
    for q in range(2):
        for kk in range(1 - q, 16):
            d = lax.rem(g + 2 * kk + q, 32)
            routes[q][kk] = remote(granules.at[d], routed.at[q, kk], s2.at[q, kk], r2.at[q, kk], {"grp": d})
            routes[q][kk].start()
    me, right, left, across, twin = neighbours()
    upper, lower, both = pl.ds(0, 16), pl.ds(16, 16), pl.ds(0, 32)

    def piece(kind, q, c, owner, rows, device):
        place = a_ref.at[q, owner, rows, pl.ds(2560 * c, 2560)]
        return remote(place, place, s3.at[kind, q, c], r3.at[kind, q, c], {"seq": device})

    def gather(kind, q, c):
        if kind < 3:
            return piece(kind, q, c, me, both, (right, left, twin)[kind])
        if kind == 3:
            return piece(3, q, c, left, upper, right)
        if kind == 4:
            return piece(4, q, c, right, lower, left)
        owner = (left, right, across, across)[kind - 5]
        return piece(kind, q, c, owner, (both, both, upper, lower)[kind - 5], twin)

    def first(q):
        for copy in routes[q].values():
            copy.wait_recv()
        if q == 0:
            own.wait()
        mine = mm(to_block, routed[q].reshape(256, HALF)).astype(BF16)
        for b in range(8):
            a_ref[q, me, :, HALF * b : HALF * b + HALF] = mine[PART * b : PART * b + PART]
        for c in range(2):
            for kind in range(3):
                gather(kind, q, c).start()

    def second(q):
        for c in range(2):
            for kind in range(2):
                gather(kind, q, c).wait_recv()
                gather(3 + kind, q, c).start()
                gather(5 + kind, q, c).start()

    def third(q):
        for c in range(2):
            for kind in range(2):
                gather(3 + kind, q, c).wait_recv()
                gather(7 + kind, q, c).start()

    first(0)
    second(0)
    first(1)
    third(0)
    second(1)
    third(1)
    for q in range(2):
        for copy in routes[q].values():
            copy.wait_send()
        for c in range(2):
            for kind in range(9):
                gather(kind, q, c).wait_send()
            for kind in (2, 5, 6, 7, 8):
                gather(kind, q, c).wait_recv()


def language(
    a_ref, w_ref, text_ref, cot_ref, gain_ref, pos_ref, attn_ref, mgain_ref, slot_ref,
    hid_ref, out_ref,
    w, text, cot, picked, proj, vis, back, ret, terms, twin_terms, far, near, summed, granules, arrived,
    w_sem, t_sem, s1, r1, s2, r2, s3, r3, s4, r4, l_sem,
):
    loads = [pltpu.make_async_copy(cot_ref, cot, t_sem.at[0])]
    for n in range(2):
        rows = pl.ds(2560 * n, 2560)
        loads.append(pltpu.make_async_copy(w_ref.at[rows], w.at[rows], w_sem.at[n]))
    loads.append(pltpu.make_async_copy(text_ref, text, t_sem.at[1]))
    for load in loads:
        load.start()
    greet(others("seq", 8) + others("grp", 32))
    me, right, left, across, twin = neighbours()
    g = lax.axis_index("grp")

    place = onehot(iota((128, ROWS), 0) == pos_ref[...])
    j = iota((ROWS, ROWS), 1)
    turned = lax.rem(g + 32 - (j % PART // 2 * 2 + j // PART), 32) * 2 + j % 2
    place = mm(place, onehot(iota((ROWS, ROWS), 0) == turned)).astype(BF16)
    pick = mm_nt(eye(ROWS), place).astype(BF16)
    taken = jnp.sum(place.astype(F32), axis=1, keepdims=True) > 0.5
    loads[0].wait()
    for c in range(8):
        picked[c] = mm(pick, cot[:, 1024 * c : 1024 * c + 1024]).astype(BF16)
    for load in loads[1:]:
        load.wait()

    def vision_part(q, k):
        d = lax.rem(me + k, 8)
        return remote(proj.at[q, d], vis.at[q, me], s1.at[q, k], r1.at[q, k], {"seq": d})

    def project(q, _):
        rows = a_ref[q].reshape(256, MERGER_FEATURES)
        for n in range(4):
            cols = slice(256 * n, 256 * n + 256)
            proj[q, :, :, cols] = mm(rows, w[:, cols]).astype(BF16).reshape(8, PART, 256)
        for k in range(1, 8):
            vision_part(q, k).start()
        vis[q, me] = proj[q, me]
        return 0

    lax.fori_loop(0, 2, project, 0)

    def back_part(q, k):
        d = lax.rem(me + k, 8)
        return remote(back.at[q, d], ret.at[q, me], s2.at[q, k], r2.at[q, k], {"seq": d})

    def gains(c):
        return gain_ref[:, pl.ds(pl.multiple_of(c * 1024, 1024), 1024)]

    scales = []
    for q in range(2):
        rows = slice(PART * q, PART * q + PART)
        for k in range(1, 8):
            vision_part(q, k).wait_recv()

        def sums(c, carry):
            v = vis[q, c].astype(F32)
            gy = picked[c, rows].astype(F32) * gains(c)
            return carry[0] + v * v, carry[1] + gy * v

        zero = jnp.zeros((PART, 1024), F32)
        squares, products = lax.fori_loop(0, 8, sums, (zero, zero))
        r = lax.rsqrt(jnp.sum(squares, axis=1, keepdims=True) / 8192.0 + EPS)
        slope = r * r * (jnp.sum(products, axis=1, keepdims=True) / 8192.0)
        scales.append(r)

        def grads(c):
            gy = picked[c, rows].astype(F32) * gains(c)
            return (r * (gy - vis[q, c].astype(F32) * slope)).astype(BF16)

        def send(k, _):
            d = lax.rem(me + k, 8)
            back[q, d] = grads(d)
            back_part(q, k).start()
            return 0

        lax.fori_loop(1, 8, send, 0)
        ret[q, me] = grads(me)

    def text_squares(c, carry):
        t = text[:, pl.ds(pl.multiple_of(c * 1024, 1024), 1024)].astype(F32)
        return carry + jnp.sum(t * t, axis=1, keepdims=True)

    r_text = lax.rsqrt(lax.fori_loop(0, 8, text_squares, jnp.zeros((128, 1), F32)) / 8192.0 + EPS)

    def hidden(c, _):
        cols = pl.ds(pl.multiple_of(c * 1024, 1024), 1024)
        gain = gains(c)
        rows = jnp.concatenate([vis[q, c].astype(F32) * scales[q] for q in range(2)], axis=0) * gain
        rows = mm(place, rows.astype(BF16))
        hid_ref[:, cols] = jnp.where(taken, rows, text[:, cols].astype(F32) * r_text * gain).astype(BF16)
        return 0

    lax.fori_loop(0, 8, hidden, 0)

    core = lax.rem(me, 2)
    x = me // 2
    chip_right, chip_left, chip_across = lax.rem(x + 1, 4), lax.rem(x + 3, 4), lax.rem(x + 2, 4)
    upper, lower = pl.ds(0, 16), pl.ds(16, 16)
    halves = pl.ds(0, 2)

    def to_twin(u):
        return remote(terms.at[u, 1 - core], twin_terms.at[u], s3.at[0, u], r3.at[0, u], {"seq": twin})

    def far_right(u):
        return remote(
            terms.at[u, core, chip_across, halves, upper], far.at[u, halves, upper],
            s3.at[1, u], r3.at[1, u], {"seq": right},
        )

    def far_left(u):
        return remote(
            terms.at[u, core, chip_across, halves, lower], far.at[u, halves, lower],
            s3.at[2, u], r3.at[2, u], {"seq": left},
        )

    def near_right(u):
        return remote(terms.at[u, core, chip_right], near.at[u, 0], s3.at[3, u], r3.at[3, u], {"seq": right})

    def near_left(u):
        return remote(terms.at[u, core, chip_left], near.at[u, 1], s3.at[4, u], r3.at[4, u], {"seq": left})

    to_granule = onehot(block_of_granule(iota((256, 256), 0)) == iota((256, 256), 1))

    def route_back(q, kk):
        d = lax.rem(g + 32 - (2 * kk + q), 32)
        return remote(granules.at[q, kk], arrived.at[g], s4.at[q, kk], r4.at[q, kk], {"grp": d})

    def send_back(q):
        rows = mm(to_granule, summed[q].reshape(256, HALF)).astype(BF16)
        granules[q] = rows.reshape(16, 16, HALF)
        if q == 0:
            arrived[g] = granules[0, 0]
        for kk in range(1 - q, 16):
            route_back(q, kk).start()

    def step(i, _):
        for q in range(2):
            @pl.when(i == 4 * q)
            def _():
                for k in range(1, 8):
                    back_part(q, k).wait_recv()

        @pl.when(i < 8)
        def _():
            u = i
            rows = pl.ds(pl.multiple_of(lax.rem(u, 4) * 1280, 1280), 1280)
            total = mm_nt(ret[u // 4].reshape(256, 1024), w[rows, :]).astype(BF16)
            for s in range(8):
                for b in range(2):
                    terms[u, s % 2, s // 2, b] = total[PART * s : PART * s + PART, HALF * b : HALF * b + HALF]
            to_twin(u).start()

        @pl.when((i >= 1) & (i < 9))
        def _():
            u = i - 1
            to_twin(u).wait_recv()
            terms[u, core] = (terms[u, core].astype(F32) + twin_terms[u].astype(F32)).astype(BF16)
            far_right(u).start()
            far_left(u).start()

        @pl.when((i >= 2) & (i < 10))
        def _():
            u = i - 2
            far_right(u).wait_recv()
            terms[u, core, chip_right, :, upper] = (
                terms[u, core, chip_right, :, upper].astype(F32) + far[u, :, upper].astype(F32)
            ).astype(BF16)
            near_right(u).start()
            far_left(u).wait_recv()
            terms[u, core, chip_left, :, lower] = (
                terms[u, core, chip_left, :, lower].astype(F32) + far[u, :, lower].astype(F32)
            ).astype(BF16)
            near_left(u).start()

        @pl.when(i >= 3)
        def _():
            u = i - 3
            near_right(u).wait_recv()
            near_left(u).wait_recv()
            total = terms[u, core, x].astype(F32) + near[u, 0].astype(F32) + near[u, 1].astype(F32)
            summed[u // 4, lax.rem(u, 4)] = total.astype(BF16)

        @pl.when(i == 6)
        def _():
            send_back(0)

        return 0

    lax.fori_loop(0, 11, step, 0)
    send_back(1)

    def settle(u, _):
        for copy in (to_twin(u), far_right(u), far_left(u), near_right(u), near_left(u)):
            copy.wait_send()
        return 0

    lax.fori_loop(0, 8, settle, 0)
    for q in range(2):
        for k in range(1, 8):
            vision_part(q, k).wait_send()
            back_part(q, k).wait_send()
    xhat, rstd = normalize(attn_ref[...].reshape(VISION_WIDTH, 256), eye(256))
    take = mm_nt(eye(512), granule_of_patch(slot_ref)).astype(BF16)
    for q in range(2):
        for kk in range(1 - q, 16):
            route_back(q, kk).wait()
    grads = mm(take, arrived[...].reshape(512, HALF))
    gy = jnp.concatenate([grads[:256], grads[256:]], axis=1) * mgain_ref[...]
    mean = jnp.mean(gy, axis=1, keepdims=True)
    along = jnp.mean(gy * xhat, axis=1, keepdims=True)
    out_ref[...] = (rstd * (gy - mean - xhat * along)).astype(BF16)


def params(collective_id=None):
    if collective_id is None:
        return pltpu.CompilerParams(vmem_limit_bytes=48 * 2**20)
    return pltpu.CompilerParams(
        vmem_limit_bytes=58 * 2**20, collective_id=collective_id, has_side_effects=True
    )


def shaped(*shape, dtype=BF16):
    return jax.ShapeDtypeStruct(shape, dtype)


def buffer(*shape):
    return pltpu.VMEM(shape, BF16)


def body(
    queries,
    key_rows,
    values,
    segment_ids,
    merger_norm_gain,
    merge_weight,
    text_rows,
    token_gain,
    cotangent,
    send_slot,
    place_pos,
):
    w = lax.all_gather(merge_weight, "grp", axis=0, tiled=True)
    gain = merger_norm_gain.reshape(1, VISION_WIDTH)
    slot = send_slot.reshape(1, ROWS)

    x = pl.pallas_call(
        heads_out,
        out_shape=shaped(8, 496, 256),
        in_specs=[VMEM] * 4,
        out_specs=VMEM,
        scratch_shapes=[buffer(8, 496, 256), DMA((8,)), DMA((8,)), DMA(())],
        compiler_params=params(1),
        name="heads_out",
    )(queries, key_rows, values, segment_ids.reshape(1, 256))
    o = pl.pallas_call(
        attention,
        out_shape=shaped(8, 160, 256),
        in_specs=[VMEM],
        out_specs=VMEM,
        scratch_shapes=[
            pltpu.VMEM((8, 2, 256, HEAD_DIM), BF16),
            pltpu.VMEM((8, 256, 128), F32),
            pltpu.VMEM((2, 8, 256, 256), F32),
        ],
        compiler_params=params(),
        name="attention",
    )(x)
    attn, a = pl.pallas_call(
        merge_and_gather,
        out_shape=[shaped(8, 160, 256), shaped(2, 8, PART, MERGER_FEATURES)],
        in_specs=[VMEM] * 3,
        out_specs=[VMEM] * 2,
        scratch_shapes=[
            buffer(32, 16, HALF),
            buffer(2, 16, 16, HALF),
            DMA((8,)),
            DMA((8,)),
            DMA((2, 16)),
            DMA((2, 16)),
            DMA(()),
            DMA((9, 2, 2)),
            DMA((9, 2, 2)),
        ],
        compiler_params=params(2),
        name="merge_and_gather",
    )(o, gain, slot)
    return pl.pallas_call(
        language,
        out_shape=[shaped(128, 8192), shaped(256, VISION_WIDTH)],
        in_specs=[VMEM] + [ANY] * 3 + [VMEM] * 5,
        out_specs=[VMEM] * 2,
        scratch_shapes=[
            buffer(MERGER_FEATURES, 1024),
            buffer(128, 8192),
            buffer(128, 8192),
            buffer(8, ROWS, 1024),
            buffer(2, 8, PART, 1024),
            buffer(2, 8, PART, 1024),
            buffer(2, 8, PART, 1024),
            buffer(2, 8, PART, 1024),
            buffer(8, 2, 4, 2, PART, HALF),
            buffer(8, 4, 2, PART, HALF),
            buffer(8, 2, PART, HALF),
            buffer(8, 2, 2, PART, HALF),
            buffer(2, 4, 2, PART, HALF),
            buffer(2, 16, 16, HALF),
            buffer(32, 16, HALF),
            DMA((2,)),
            DMA((2,)),
            DMA((2, 8)),
            DMA((2, 8)),
            DMA((2, 8)),
            DMA((2, 8)),
            DMA((5, 8)),
            DMA((5, 8)),
            DMA((2, 16)),
            DMA((2, 16)),
            DMA(()),
        ],
        compiler_params=params(3),
        name="language",
    )(
        a,
        w,
        text_rows,
        cotangent,
        token_gain.reshape(1, 8192),
        place_pos.reshape(1, ROWS),
        attn,
        gain,
        slot,
    )


def solution(mesh):
    in_specs = (
        P(("grp", "seq"), None),
        P(("grp", "seq"), None),
        P(("grp", "seq"), None),
        P(("grp", "seq")),
        P(),
        P("grp", "seq"),
        P(("grp", "seq"), None),
        P(),
        P(("grp", "seq"), None),
        P(("grp", "seq")),
        P(("grp", "seq")),
    )
    out_specs = (P(("grp", "seq"), None), P(("grp", "seq"), None))
    return jax.shard_map(body, mesh=mesh, in_specs=in_specs, out_specs=out_specs, check_vma=False)
```

```python
import jax
import jax.numpy as jnp
from jax import lax
from jax.experimental import pallas as pl
from jax.experimental.pallas import tpu as pltpu
from jax.sharding import PartitionSpec as P

VISION_WIDTH = 1280
HEAD_DIM = 80
MERGER_FEATURES = 5120
ROWS = 64
PART = 32
HALF = 640
EPS = 1e-06
NT = (((1,), (1,)), ((), ()))
F32 = jnp.float32
BF16 = jnp.bfloat16
LOG2E = 1.4426950408889634
MESH = pl.DeviceIdType.MESH
DMA = pltpu.SemaphoreType.DMA
ANY = pl.BlockSpec(memory_space=pl.ANY)
VMEM = pl.BlockSpec(memory_space=pltpu.VMEM)


def iota(shape, axis):
    return lax.broadcasted_iota(jnp.int32, shape, axis)


def eye(n):
    return (iota((n, n), 0) == iota((n, n), 1)).astype(F32).astype(BF16)


def mm(a, b):
    return jnp.dot(a, b, preferred_element_type=F32)


def mm_nt(a, b):
    return lax.dot_general(a, b, NT, preferred_element_type=F32)


def onehot(mask):
    return mask.astype(F32).astype(BF16)


def block_of_granule(rho):
    kk, half, i, p = rho // 16, rho // 8 % 2, rho // 4 % 2, rho % 4
    return (p * 2 + half) * PART + kk * 2 + i


def attention(x_ref, o_ref, k_scr, idk_scr, s_scr):
    one = eye(256)
    scale = HEAD_DIM ** (-0.5) * LOG2E
    first, last, id_rows = [], [], []
    for j in range(8):
        for h in range(2):
            k_scr[j, h] = mm_nt(one, x_ref[j, 160 + 80 * h : 240 + 80 * h, :]).astype(BF16)
        parts = x_ref[j, 480:496, :]
        cols = mm_nt(one, parts)
        idk_scr[j] = jnp.broadcast_to(cols[:, 0:1] * 16.0 + cols[:, 1:2], (256, 128))
        parts = parts.astype(F32)
        row = parts[0:1] * 16.0 + parts[1:2]
        first.append(jnp.min(row))
        last.append(jnp.max(row))
    for i in range(8):
        parts = x_ref[i, 480:496, :].astype(F32)
        idq = parts[0:1] * 16.0 + parts[1:2]
        lo, hi = jnp.int32(0), jnp.int32(8)
        for j in range(8):
            if j < i:
                lo = lo + jnp.where(last[j] < first[i], 1, 0)
            if j > i:
                hi = hi - jnp.where(first[j] > last[i], 1, 0)

        def scores(j, m):
            idk = idk_scr[j]
            same = jnp.concatenate([idk, idk], axis=1) == idq
            new = []
            for h in range(2):
                s = mm(k_scr[j, h], x_ref[i, 80 * h : 80 * h + 80, :])
                s = jnp.where(same, s, -1e30)
                s_scr[h, j] = s
                new.append(jnp.maximum(m[h], jnp.max(s.reshape(32, 8, 256), axis=0)))
            return tuple(new)

        m = lax.fori_loop(lo, hi, scores, (jnp.full((8, 256), -1e30, F32),) * 2)
        top = [jnp.max(m[h], axis=0, keepdims=True) for h in range(2)]

        def weighted(j, carry):
            new = []
            for h in range(2):
                acc, total = carry[h]
                p = jnp.exp2((s_scr[h, j] - top[h]) * scale)
                total = total + jnp.sum(p.reshape(32, 8, 256), axis=0)
                acc = acc + mm(x_ref[j, 320 + 80 * h : 400 + 80 * h, :], p.astype(BF16))
                new.append((acc, total))
            return tuple(new)

        zero = (jnp.zeros((HEAD_DIM, 256), F32), jnp.zeros((8, 256), F32))
        done = lax.fori_loop(lo, hi, weighted, (zero, zero))
        for h in range(2):
            acc, total = done[h]
            total = jnp.sum(total, axis=0, keepdims=True)
            o_ref[i, 80 * h : 80 * h + 80, :] = (acc / total).astype(BF16)


def normalize(attn_t, one):
    x = jnp.concatenate([mm_nt(one, attn_t[256 * f : 256 * f + 256, :]) for f in range(5)], axis=1)
    x = x - jnp.mean(x, axis=1, keepdims=True)
    rstd = lax.rsqrt(jnp.mean(x * x, axis=1, keepdims=True) + EPS)
    return x * rstd, rstd


def greet(devices):
    barrier = pltpu.get_barrier_semaphore()
    for device in devices:
        pl.semaphore_signal(barrier, inc=1, device_id=device, device_id_type=MESH)
    pl.semaphore_wait(barrier, len(devices))


def remote(src, dst, send_sem, recv_sem, device):
    return pltpu.make_async_remote_copy(
        src_ref=src, dst_ref=dst, send_sem=send_sem, recv_sem=recv_sem, device_id=device, device_id_type=MESH
    )


def others(axis, n):
    me = lax.axis_index(axis)
    return [{axis: lax.rem(me + k, n)} for k in range(1, n)]


def sub_block_of_granule(rho):
    n, half, i, p = rho // 16, rho // 8 % 2, rho // 4 % 2, rho % 4
    return (p * 2 + half) * 16 + n * 2 + i


def exchange(src, dst, send_sem, recv_sem, local_sem):
    me = lax.axis_index("seq")
    copies = []
    for k in range(1, 8):
        d = lax.rem(me + k, 8)
        copy = remote(src.at[d], dst.at[me], send_sem.at[k], recv_sem.at[k], {"seq": d})
        copy.start()
        copies.append(copy)
    own = pltpu.make_async_copy(src.at[me], dst.at[me], local_sem)
    own.start()
    return copies + [own]


def finish(copies):
    for copy in copies:
        copy.wait()


def heads_out(
    q_ref, k_ref, v_ref, ids_ref, out_ref, parts, send_sem, recv_sem, local_sem
):
    one = eye(256)
    greet(others("seq", 8))
    ids = ids_ref[...]
    rows = jnp.where(iota((16, 256), 0) % 2 == 0, ids // 16, ids % 16)
    rows = rows.astype(F32).astype(BF16)
    for dev in range(8):
        parts[dev, 480:496, :] = rows
    for t, ref in enumerate((q_ref, k_ref, v_ref)):
        for f in range(5):
            block = mm_nt(one, ref[:, 256 * f : 256 * f + 256]).astype(BF16)
            lower = 256 * f
            while lower < 256 * f + 256:
                dev = lower // 160
                upper = min(160 * (dev + 1), 256 * f + 256)
                parts[dev, 160 * t + lower - 160 * dev : 160 * t + upper - 160 * dev, :] = block[
                    lower - 256 * f : upper - 256 * f, :
                ]
                lower = upper
    finish(exchange(parts, out_ref, send_sem, recv_sem, local_sem))


def neighbours():
    me = lax.axis_index("seq")
    x, core = me // 2, lax.rem(me, 2)
    chip = lambda k: lax.rem(x + k, 4) * 2 + core
    return me, chip(1), chip(3), chip(2), x * 2 + 1 - core


def granule_of_patch(slot_ref):
    slot = jnp.broadcast_to(slot_ref[...], (8, ROWS)).astype(F32).astype(BF16)
    repeat = onehot(iota((ROWS, 512), 0) == iota((ROWS, 512), 1) % 256 // 4)
    slot = mm(slot, repeat)[0:1].astype(jnp.int32)
    kappa = iota((1, 512), 1)
    target = slot // 2 * 16 + kappa // 256 * 8 + slot % 2 * 4 + kappa % 4
    return onehot(iota((512, 512), 0) == target)


def merge_and_gather(
    o_ref, gain_ref, slot_ref, attn_ref, a_ref, granules, routed, s1, r1, s2, r2, l_sem, s3, r3
):
    greet(others("seq", 8) + others("grp", 32))
    copies = exchange(o_ref, attn_ref, s1, r1, l_sem)
    g = lax.axis_index("grp")
    move = granule_of_patch(slot_ref)
    to_block = onehot(iota((256, 256), 0) == block_of_granule(iota((256, 256), 1)))
    finish(copies)
    xhat, _ = normalize(attn_ref[...].reshape(VISION_WIDTH, 256), eye(256))
    merged = (xhat * gain_ref[...]).astype(BF16)
    stacked = jnp.concatenate([merged[:, :HALF], merged[:, HALF:]], axis=0)
    granules[...] = mm(move, stacked).astype(BF16).reshape(32, 16, HALF)

    own = pltpu.make_async_copy(granules.at[g], routed.at[0, 0], l_sem)
    own.start()
    routes = [{}, {}]
    for q in range(2):
        for kk in range(1 - q, 16):
            d = lax.rem(g + 2 * kk + q, 32)
            routes[q][kk] = remote(granules.at[d], routed.at[q, kk], s2.at[q, kk], r2.at[q, kk], {"grp": d})
            routes[q][kk].start()
    me, right, left, across, twin = neighbours()
    upper, lower, both = pl.ds(0, 16), pl.ds(16, 16), pl.ds(0, 32)

    def piece(kind, q, c, owner, rows, device):
        place = a_ref.at[q, owner, rows, pl.ds(2560 * c, 2560)]
        return remote(place, place, s3.at[kind, q, c], r3.at[kind, q, c], {"seq": device})

    def gather(kind, q, c):
        if kind < 3:
            return piece(kind, q, c, me, both, (right, left, twin)[kind])
        if kind == 3:
            return piece(3, q, c, left, upper, right)
        if kind == 4:
            return piece(4, q, c, right, lower, left)
        owner = (left, right, across, across)[kind - 5]
        return piece(kind, q, c, owner, (both, both, upper, lower)[kind - 5], twin)

    def first(q):
        for copy in routes[q].values():
            copy.wait_recv()
        if q == 0:
            own.wait()
        mine = mm(to_block, routed[q].reshape(256, HALF)).astype(BF16)
        for b in range(8):
            a_ref[q, me, :, HALF * b : HALF * b + HALF] = mine[PART * b : PART * b + PART]
        for c in range(2):
            for kind in range(3):
                gather(kind, q, c).start()

    def second(q):
        for c in range(2):
            for kind in range(2):
                gather(kind, q, c).wait_recv()
                gather(3 + kind, q, c).start()
                gather(5 + kind, q, c).start()

    def third(q):
        for c in range(2):
            for kind in range(2):
                gather(3 + kind, q, c).wait_recv()
                gather(7 + kind, q, c).start()

    first(0)
    second(0)
    first(1)
    third(0)
    second(1)
    third(1)
    for q in range(2):
        for copy in routes[q].values():
            copy.wait_send()
        for c in range(2):
            for kind in range(9):
                gather(kind, q, c).wait_send()
            for kind in (2, 5, 6, 7, 8):
                gather(kind, q, c).wait_recv()


def language(
    a_ref, w_ref, text_ref, cot_ref, gain_ref, pos_ref, attn_ref, mgain_ref, slot_ref,
    hid_ref, out_ref,
    a, w, text, cot, picked, proj, vis, back, ret, terms, twin_terms, far, near, summed, granules, arrived,
    w_sem, t_sem, s1, r1, s2, r2, s3, r3, s4, r4, l_sem,
):
    def load_w(n):
        cols = pl.ds(pl.multiple_of(n * 256, 256), 256)
        return pltpu.make_async_copy(w_ref.at[:, cols], w.at[:, cols], w_sem.at[n])

    load_cot = pltpu.make_async_copy(cot_ref, cot, t_sem.at[0])
    load_text = pltpu.make_async_copy(text_ref, text, t_sem.at[1])
    load_a = pltpu.make_async_copy(a_ref, a, t_sem.at[2])
    load_a.start()
    for n in range(4):
        load_w(n).start()
    load_cot.start()
    load_text.start()
    greet(others("seq", 8) + others("grp", 32))
    me, right, left, across, twin = neighbours()
    g = lax.axis_index("grp")

    place = onehot(iota((128, ROWS), 0) == pos_ref[...])
    j = iota((ROWS, ROWS), 1)
    turned = lax.rem(g + 32 - (j % PART // 2 * 2 + j // PART), 32) * 2 + j % 2
    place = mm(place, onehot(iota((ROWS, ROWS), 0) == turned)).astype(BF16)
    pick = mm_nt(eye(ROWS), place).astype(BF16)
    taken = jnp.sum(place.astype(F32), axis=1, keepdims=True) > 0.5
    load_a.wait()

    def vision_tile(n, k):
        d = lax.rem(me + k, 8)
        return remote(proj.at[n, d], vis.at[n, me], s1.at[n, k], r1.at[n, k], {"seq": d})

    def project(n, _):
        load_w(n).wait()
        cols = pl.ds(pl.multiple_of(n * 256, 256), 256)
        total = mm(a[...].reshape(512, MERGER_FEATURES), w[:, cols]).astype(BF16)
        for q in range(2):
            for d in range(8):
                row = PART * (8 * q + d)
                proj[n, d, q] = total[row : row + PART]
        for k in range(1, 8):
            vision_tile(n, k).start()
        vis[n, me] = proj[n, me]
        return 0

    lax.fori_loop(0, 4, project, 0)
    load_cot.wait()
    for c in range(8):
        for n in range(4):
            picked[n, c] = mm(pick, cot[:, 1024 * c + 256 * n : 1024 * c + 256 * n + 256]).astype(BF16)
    load_text.wait()

    def back_part(q, k):
        d = lax.rem(me + k, 8)
        return remote(back.at[q, d], ret.at[q, me], s2.at[q, k], r2.at[q, k], {"seq": d})

    def gains(c, n):
        return gain_ref[:, pl.ds(pl.multiple_of(c * 1024 + n * 256, 256), 256)]

    def text_squares(c, carry):
        t = text[:, pl.ds(pl.multiple_of(c * 1024, 1024), 1024)].astype(F32)
        return carry + jnp.sum(t * t, axis=1, keepdims=True)

    r_text = lax.rsqrt(lax.fori_loop(0, 8, text_squares, jnp.zeros((128, 1), F32)) / 8192.0 + EPS)

    def tile_sums(n, carry):
        for k in range(1, 8):
            vision_tile(n, k).wait_recv()

        def sums(c, carry):
            v = vis[n, c].reshape(ROWS, 256).astype(F32)
            gy = picked[n, c].astype(F32) * gains(c, n)
            return carry[0] + v * v, carry[1] + gy * v

        return lax.fori_loop(0, 8, sums, carry)

    zero = jnp.zeros((ROWS, 256), F32)
    squares, products = lax.fori_loop(0, 4, tile_sums, (zero, zero))
    r = lax.rsqrt(jnp.sum(squares, axis=1, keepdims=True) / 8192.0 + EPS)
    slope = r * r * (jnp.sum(products, axis=1, keepdims=True) / 8192.0)

    for q in range(2):
        rows = slice(PART * q, PART * q + PART)

        def grads(c, ref):
            for n in range(4):
                gy = picked[n, c, rows].astype(F32) * gains(c, n)
                grad = r[rows] * (gy - vis[n, c, q].astype(F32) * slope[rows])
                ref[:, 256 * n : 256 * n + 256] = grad.astype(BF16)

        def send(k, _):
            d = lax.rem(me + k, 8)
            grads(d, back.at[q, d])
            back_part(q, k).start()
            return 0

        lax.fori_loop(1, 8, send, 0)
        grads(me, ret.at[q, me])

    def hidden(c):
        for n in range(4):
            cols = pl.ds(pl.multiple_of(c * 1024 + n * 256, 256), 256)
            gain = gains(c, n)
            rows = (vis[n, c].reshape(ROWS, 256).astype(F32) * r * gain).astype(BF16)
            own = (text[:, cols].astype(F32) * r_text * gain).astype(BF16)
            hid_ref[:, cols] = jnp.where(taken, mm(place, rows), own.astype(F32)).astype(BF16)

    core = lax.rem(me, 2)
    x = me // 2
    chip_right, chip_left, chip_across = lax.rem(x + 1, 4), lax.rem(x + 3, 4), lax.rem(x + 2, 4)
    upper, lower = pl.ds(0, 2), pl.ds(2, 2)

    def to_twin(u):
        return remote(terms.at[u, 1 - core], twin_terms.at[u], s3.at[0, u], r3.at[0, u], {"seq": twin})

    def far_right(u):
        return remote(
            terms.at[u, core, chip_across, upper], far.at[u, upper], s3.at[1, u], r3.at[1, u], {"seq": right}
        )

    def far_left(u):
        return remote(
            terms.at[u, core, chip_across, lower], far.at[u, lower], s3.at[2, u], r3.at[2, u], {"seq": left}
        )

    def near_right(u):
        return remote(terms.at[u, core, chip_right], near.at[u, 0], s3.at[3, u], r3.at[3, u], {"seq": right})

    def near_left(u):
        return remote(terms.at[u, core, chip_left], near.at[u, 1], s3.at[4, u], r3.at[4, u], {"seq": left})

    to_granule = onehot(sub_block_of_granule(iota((128, 128), 0)) == iota((128, 128), 1))

    def route_back(t, n):
        d = lax.rem(g + 32 - (2 * (t % 2 * 8 + n) + t // 2), 32)
        return remote(granules.at[t, n], arrived.at[g], s4.at[t, n], r4.at[t, n], {"grp": d})

    def send_back(t):
        rows = mm(to_granule, summed[t].reshape(128, HALF)).astype(BF16)
        granules[t] = rows.reshape(8, 16, HALF)
        if t == 0:
            arrived[g] = granules[0, 0]
        for n in range(1 if t == 0 else 0, 8):
            route_back(t, n).start()

    def step(i, _):
        for q in range(2):
            @pl.when(i == 4 * q)
            def _():
                for k in range(1, 8):
                    back_part(q, k).wait_recv()

        @pl.when(i < 8)
        def _():
            u = i
            rows = pl.ds(pl.multiple_of(lax.rem(u, 2) * 2560, 2560), 2560)
            own = pl.ds(pl.multiple_of(lax.rem(u // 2, 2) * 16, 16), 16)
            total = mm_nt(ret[u // 4, :, own, :].reshape(128, 1024), w[rows, :]).astype(BF16)
            for s in range(8):
                for b in range(4):
                    terms[u, s % 2, s // 2, b] = total[16 * s : 16 * s + 16, HALF * b : HALF * b + HALF]
            to_twin(u).start()
            hidden(u)

        @pl.when((i >= 1) & (i < 9))
        def _():
            u = i - 1
            to_twin(u).wait_recv()
            terms[u, core] = (terms[u, core].astype(F32) + twin_terms[u].astype(F32)).astype(BF16)
            far_right(u).start()
            far_left(u).start()

        @pl.when((i >= 2) & (i < 10))
        def _():
            u = i - 2
            far_right(u).wait_recv()
            terms[u, core, chip_right, upper] = (
                terms[u, core, chip_right, upper].astype(F32) + far[u, upper].astype(F32)
            ).astype(BF16)
            near_right(u).start()
            far_left(u).wait_recv()
            terms[u, core, chip_left, lower] = (
                terms[u, core, chip_left, lower].astype(F32) + far[u, lower].astype(F32)
            ).astype(BF16)
            near_left(u).start()

        @pl.when(i >= 3)
        def _():
            u = i - 3
            near_right(u).wait_recv()
            near_left(u).wait_recv()
            total = terms[u, core, x].astype(F32) + near[u, 0].astype(F32) + near[u, 1].astype(F32)
            summed[u // 2, lax.rem(u, 2)] = total.astype(BF16)

        for t in range(3):
            @pl.when(i == 2 * t + 4)
            def _():
                send_back(t)

        return 0

    lax.fori_loop(0, 11, step, 0)
    send_back(3)

    def settle(u, _):
        for copy in (to_twin(u), far_right(u), far_left(u), near_right(u), near_left(u)):
            copy.wait_send()
        return 0

    lax.fori_loop(0, 8, settle, 0)
    for q in range(2):
        for k in range(1, 8):
            back_part(q, k).wait_send()
    for n in range(4):
        for k in range(1, 8):
            vision_tile(n, k).wait_send()
    xhat, rstd = normalize(attn_ref[...].reshape(VISION_WIDTH, 256), eye(256))
    take = mm_nt(eye(512), granule_of_patch(slot_ref)).astype(BF16)
    for t in range(4):
        for n in range(1 if t == 0 else 0, 8):
            route_back(t, n).wait()
    grads = mm(take, arrived[...].reshape(512, HALF))
    gy = jnp.concatenate([grads[:256], grads[256:]], axis=1) * mgain_ref[...]
    mean = jnp.mean(gy, axis=1, keepdims=True)
    along = jnp.mean(gy * xhat, axis=1, keepdims=True)
    out_ref[...] = (rstd * (gy - mean - xhat * along)).astype(BF16)


def params(collective_id=None):
    if collective_id is None:
        return pltpu.CompilerParams(vmem_limit_bytes=48 * 2**20)
    return pltpu.CompilerParams(
        vmem_limit_bytes=58 * 2**20, collective_id=collective_id, has_side_effects=True
    )


def shaped(*shape, dtype=BF16):
    return jax.ShapeDtypeStruct(shape, dtype)


def buffer(*shape):
    return pltpu.VMEM(shape, BF16)


def body(
    queries,
    key_rows,
    values,
    segment_ids,
    merger_norm_gain,
    merge_weight,
    text_rows,
    token_gain,
    cotangent,
    send_slot,
    place_pos,
):
    w = lax.all_gather(merge_weight, "grp", axis=0, tiled=True)
    gain = merger_norm_gain.reshape(1, VISION_WIDTH)
    slot = send_slot.reshape(1, ROWS)

    x = pl.pallas_call(
        heads_out,
        out_shape=shaped(8, 496, 256),
        in_specs=[VMEM] * 4,
        out_specs=VMEM,
        scratch_shapes=[buffer(8, 496, 256), DMA((8,)), DMA((8,)), DMA(())],
        compiler_params=params(1),
        name="heads_out",
    )(queries, key_rows, values, segment_ids.reshape(1, 256))
    o = pl.pallas_call(
        attention,
        out_shape=shaped(8, 160, 256),
        in_specs=[VMEM],
        out_specs=VMEM,
        scratch_shapes=[
            pltpu.VMEM((8, 2, 256, HEAD_DIM), BF16),
            pltpu.VMEM((8, 256, 128), F32),
            pltpu.VMEM((2, 8, 256, 256), F32),
        ],
        compiler_params=params(),
        name="attention",
    )(x)
    attn, a = pl.pallas_call(
        merge_and_gather,
        out_shape=[shaped(8, 160, 256), shaped(2, 8, PART, MERGER_FEATURES)],
        in_specs=[VMEM] * 3,
        out_specs=[VMEM] * 2,
        scratch_shapes=[
            buffer(32, 16, HALF),
            buffer(2, 16, 16, HALF),
            DMA((8,)),
            DMA((8,)),
            DMA((2, 16)),
            DMA((2, 16)),
            DMA(()),
            DMA((9, 2, 2)),
            DMA((9, 2, 2)),
        ],
        compiler_params=params(2),
        name="merge_and_gather",
    )(o, gain, slot)
    return pl.pallas_call(
        language,
        out_shape=[shaped(128, 8192), shaped(256, VISION_WIDTH)],
        in_specs=[ANY] * 4 + [VMEM] * 5,
        out_specs=[VMEM] * 2,
        scratch_shapes=[
            buffer(2, 8, PART, MERGER_FEATURES),
            buffer(MERGER_FEATURES, 1024),
            buffer(128, 8192),
            buffer(128, 8192),
            buffer(4, 8, ROWS, 256),
            buffer(4, 8, 2, PART, 256),
            buffer(4, 8, 2, PART, 256),
            buffer(2, 8, PART, 1024),
            buffer(2, 8, PART, 1024),
            buffer(8, 2, 4, 4, 16, HALF),
            buffer(8, 4, 4, 16, HALF),
            buffer(8, 4, 16, HALF),
            buffer(8, 2, 4, 16, HALF),
            buffer(4, 2, 4, 16, HALF),
            buffer(4, 8, 16, HALF),
            buffer(32, 16, HALF),
            DMA((4,)),
            DMA((3,)),
            DMA((4, 8)),
            DMA((4, 8)),
            DMA((2, 8)),
            DMA((2, 8)),
            DMA((5, 8)),
            DMA((5, 8)),
            DMA((4, 8)),
            DMA((4, 8)),
            DMA(()),
        ],
        compiler_params=params(3),
        name="language",
    )(
        a,
        w,
        text_rows,
        cotangent,
        token_gain.reshape(1, 8192),
        place_pos.reshape(1, ROWS),
        attn,
        gain,
        slot,
    )


def solution(mesh):
    in_specs = (
        P(("grp", "seq"), None),
        P(("grp", "seq"), None),
        P(("grp", "seq"), None),
        P(("grp", "seq")),
        P(),
        P("grp", "seq"),
        P(("grp", "seq"), None),
        P(),
        P(("grp", "seq"), None),
        P(("grp", "seq")),
        P(("grp", "seq")),
    )
    out_specs = (P(("grp", "seq"), None), P(("grp", "seq"), None))
    return jax.shard_map(body, mesh=mesh, in_specs=in_specs, out_specs=out_specs, check_vma=False)
```

```python
import jax
import jax.numpy as jnp
from jax import lax
from jax.experimental import pallas as pl
from jax.experimental.pallas import tpu as pltpu
from jax.sharding import PartitionSpec as P

VISION_WIDTH = 1280
HEAD_DIM = 80
MERGER_FEATURES = 5120
ROWS = 64
PART = 32
HALF = 640
EPS = 1e-06
NT = (((1,), (1,)), ((), ()))
F32 = jnp.float32
BF16 = jnp.bfloat16
LOG2E = 1.4426950408889634
MESH = pl.DeviceIdType.MESH
DMA = pltpu.SemaphoreType.DMA
ANY = pl.BlockSpec(memory_space=pl.ANY)
VMEM = pl.BlockSpec(memory_space=pltpu.VMEM)


def iota(shape, axis):
    return lax.broadcasted_iota(jnp.int32, shape, axis)


def eye(n):
    return (iota((n, n), 0) == iota((n, n), 1)).astype(F32).astype(BF16)


def mm(a, b):
    return jnp.dot(a, b, preferred_element_type=F32)


def mm_nt(a, b):
    return lax.dot_general(a, b, NT, preferred_element_type=F32)


def onehot(mask):
    return mask.astype(F32).astype(BF16)


def block_of_granule(rho):
    kk, half, i, p = rho // 16, rho // 8 % 2, rho // 4 % 2, rho % 4
    return (p * 2 + half) * PART + kk * 2 + i


def attention(x_ref, o_ref, k_scr, idk_scr, s_scr):
    one = eye(256)
    scale = HEAD_DIM ** (-0.5) * LOG2E
    first, last, id_rows = [], [], []
    for j in range(8):
        for h in range(2):
            k_scr[j, h] = mm_nt(one, x_ref[j, 160 + 80 * h : 240 + 80 * h, :]).astype(BF16)
        parts = x_ref[j, 480:496, :]
        cols = mm_nt(one, parts)
        idk_scr[j] = jnp.broadcast_to(cols[:, 0:1] * 16.0 + cols[:, 1:2], (256, 128))
        parts = parts.astype(F32)
        row = parts[0:1] * 16.0 + parts[1:2]
        first.append(jnp.min(row))
        last.append(jnp.max(row))
    for i in range(8):
        parts = x_ref[i, 480:496, :].astype(F32)
        idq = parts[0:1] * 16.0 + parts[1:2]
        lo, hi = jnp.int32(0), jnp.int32(8)
        for j in range(8):
            if j < i:
                lo = lo + jnp.where(last[j] < first[i], 1, 0)
            if j > i:
                hi = hi - jnp.where(first[j] > last[i], 1, 0)

        def scores(j, m):
            idk = idk_scr[j]
            same = jnp.concatenate([idk, idk], axis=1) == idq
            new = []
            for h in range(2):
                s = mm(k_scr[j, h], x_ref[i, 80 * h : 80 * h + 80, :])
                s = jnp.where(same, s, -1e30)
                s_scr[h, j] = s
                new.append(jnp.maximum(m[h], jnp.max(s.reshape(32, 8, 256), axis=0)))
            return tuple(new)

        m = lax.fori_loop(lo, hi, scores, (jnp.full((8, 256), -1e30, F32),) * 2)
        top = [jnp.max(m[h], axis=0, keepdims=True) for h in range(2)]

        def weighted(j, carry):
            new = []
            for h in range(2):
                acc, total = carry[h]
                p = jnp.exp2((s_scr[h, j] - top[h]) * scale)
                total = total + jnp.sum(p.reshape(32, 8, 256), axis=0)
                acc = acc + mm(x_ref[j, 320 + 80 * h : 400 + 80 * h, :], p.astype(BF16))
                new.append((acc, total))
            return tuple(new)

        zero = (jnp.zeros((HEAD_DIM, 256), F32), jnp.zeros((8, 256), F32))
        done = lax.fori_loop(lo, hi, weighted, (zero, zero))
        for h in range(2):
            acc, total = done[h]
            total = jnp.sum(total, axis=0, keepdims=True)
            o_ref[i, 80 * h : 80 * h + 80, :] = (acc / total).astype(BF16)


def normalize(attn_t, one):
    x = jnp.concatenate([mm_nt(one, attn_t[256 * f : 256 * f + 256, :]) for f in range(5)], axis=1)
    x = x - jnp.mean(x, axis=1, keepdims=True)
    rstd = lax.rsqrt(jnp.mean(x * x, axis=1, keepdims=True) + EPS)
    return x * rstd, rstd


def greet(devices):
    barrier = pltpu.get_barrier_semaphore()
    for device in devices:
        pl.semaphore_signal(barrier, inc=1, device_id=device, device_id_type=MESH)
    pl.semaphore_wait(barrier, len(devices))


def remote(src, dst, send_sem, recv_sem, device):
    return pltpu.make_async_remote_copy(
        src_ref=src, dst_ref=dst, send_sem=send_sem, recv_sem=recv_sem, device_id=device, device_id_type=MESH
    )


def others(axis, n):
    me = lax.axis_index(axis)
    return [{axis: lax.rem(me + k, n)} for k in range(1, n)]


def sub_block_of_granule(rho):
    n, half, i, p = rho // 16, rho // 8 % 2, rho // 4 % 2, rho % 4
    return (p * 2 + half) * 16 + n * 2 + i


def exchange(src, dst, send_sem, recv_sem, local_sem):
    me = lax.axis_index("seq")
    copies = []
    for k in range(1, 8):
        d = lax.rem(me + k, 8)
        copy = remote(src.at[d], dst.at[me], send_sem.at[k], recv_sem.at[k], {"seq": d})
        copy.start()
        copies.append(copy)
    own = pltpu.make_async_copy(src.at[me], dst.at[me], local_sem)
    own.start()
    return copies + [own]


def finish(copies):
    for copy in copies:
        copy.wait()


def heads_out(
    q_ref, k_ref, v_ref, ids_ref, out_ref, parts, send_sem, recv_sem, local_sem
):
    one = eye(256)
    greet(others("seq", 8))
    ids = ids_ref[...]
    rows = jnp.where(iota((16, 256), 0) % 2 == 0, ids // 16, ids % 16)
    rows = rows.astype(F32).astype(BF16)
    for dev in range(8):
        parts[dev, 480:496, :] = rows
    for t, ref in enumerate((q_ref, k_ref, v_ref)):
        for f in range(5):
            block = mm_nt(one, ref[:, 256 * f : 256 * f + 256]).astype(BF16)
            lower = 256 * f
            while lower < 256 * f + 256:
                dev = lower // 160
                upper = min(160 * (dev + 1), 256 * f + 256)
                parts[dev, 160 * t + lower - 160 * dev : 160 * t + upper - 160 * dev, :] = block[
                    lower - 256 * f : upper - 256 * f, :
                ]
                lower = upper
    finish(exchange(parts, out_ref, send_sem, recv_sem, local_sem))


def neighbours():
    me = lax.axis_index("seq")
    x, core = me // 2, lax.rem(me, 2)
    chip = lambda k: lax.rem(x + k, 4) * 2 + core
    return me, chip(1), chip(3), chip(2), x * 2 + 1 - core


def granule_of_patch(slot_ref):
    slot = jnp.broadcast_to(slot_ref[...], (8, ROWS)).astype(F32).astype(BF16)
    repeat = onehot(iota((ROWS, 512), 0) == iota((ROWS, 512), 1) % 256 // 4)
    slot = mm(slot, repeat)[0:1].astype(jnp.int32)
    kappa = iota((1, 512), 1)
    target = slot // 2 * 16 + kappa // 256 * 8 + slot % 2 * 4 + kappa % 4
    return onehot(iota((512, 512), 0) == target)


def merge_and_gather(
    o_ref, gain_ref, slot_ref, attn_ref, a_ref, granules, routed, s1, r1, s2, r2, l_sem, s3, r3
):
    greet(others("seq", 8) + others("grp", 32))
    copies = exchange(o_ref, attn_ref, s1, r1, l_sem)
    g = lax.axis_index("grp")
    move = granule_of_patch(slot_ref)
    to_block = onehot(iota((256, 256), 0) == block_of_granule(iota((256, 256), 1)))
    finish(copies)
    xhat, _ = normalize(attn_ref[...].reshape(VISION_WIDTH, 256), eye(256))
    merged = (xhat * gain_ref[...]).astype(BF16)
    stacked = jnp.concatenate([merged[:, :HALF], merged[:, HALF:]], axis=0)
    granules[...] = mm(move, stacked).astype(BF16).reshape(32, 16, HALF)

    own = pltpu.make_async_copy(granules.at[g], routed.at[0, 0], l_sem)
    own.start()
    routes = [{}, {}]
    for q in range(2):
        for kk in range(1 - q, 16):
            d = lax.rem(g + 2 * kk + q, 32)
            routes[q][kk] = remote(granules.at[d], routed.at[q, kk], s2.at[q, kk], r2.at[q, kk], {"grp": d})
            routes[q][kk].start()
    me, right, left, across, twin = neighbours()
    upper, lower, both = pl.ds(0, 16), pl.ds(16, 16), pl.ds(0, 32)

    def piece(kind, q, c, owner, rows, device):
        place = a_ref.at[q, owner, rows, pl.ds(2560 * c, 2560)]
        return remote(place, place, s3.at[kind, q, c], r3.at[kind, q, c], {"seq": device})

    def gather(kind, q, c):
        if kind < 3:
            return piece(kind, q, c, me, both, (right, left, twin)[kind])
        if kind == 3:
            return piece(3, q, c, left, upper, right)
        if kind == 4:
            return piece(4, q, c, right, lower, left)
        owner = (left, right, across, across)[kind - 5]
        return piece(kind, q, c, owner, (both, both, upper, lower)[kind - 5], twin)

    def first(q):
        for copy in routes[q].values():
            copy.wait_recv()
        if q == 0:
            own.wait()
        mine = mm(to_block, routed[q].reshape(256, HALF)).astype(BF16)
        for b in range(8):
            a_ref[q, me, :, HALF * b : HALF * b + HALF] = mine[PART * b : PART * b + PART]
        for c in range(2):
            for kind in range(3):
                gather(kind, q, c).start()

    def second(q):
        for c in range(2):
            for kind in range(2):
                gather(kind, q, c).wait_recv()
                gather(3 + kind, q, c).start()
                gather(5 + kind, q, c).start()

    def third(q):
        for c in range(2):
            for kind in range(2):
                gather(3 + kind, q, c).wait_recv()
                gather(7 + kind, q, c).start()

    first(0)
    second(0)
    first(1)
    third(0)
    second(1)
    third(1)
    for q in range(2):
        for copy in routes[q].values():
            copy.wait_send()
        for c in range(2):
            for kind in range(9):
                gather(kind, q, c).wait_send()
            for kind in (2, 5, 6, 7, 8):
                gather(kind, q, c).wait_recv()


def language(
    a_ref, w_ref, text_ref, cot_ref, gain_ref, pos_ref, attn_ref, mgain_ref, slot_ref,
    hid_ref, out_ref,
    a, w, text, cot, picked, proj, vis, back, ret, terms, twin_terms, far, near, summed, granules, arrived,
    w_sem, t_sem, s1, r1, s2, r2, s3, r3, s4, r4, h_sem, attn,
):
    def load_w(n):
        cols = pl.ds(pl.multiple_of(n * 256, 256), 256)
        return pltpu.make_async_copy(w_ref.at[:, cols], w.at[:, cols], w_sem.at[n])

    load_cot = pltpu.make_async_copy(cot_ref, cot, t_sem.at[0])
    load_text = pltpu.make_async_copy(text_ref, text, t_sem.at[1])
    load_a = pltpu.make_async_copy(a_ref, a, t_sem.at[2])
    load_a.start()
    for n in range(4):
        load_w(n).start()
    load_cot.start()
    load_text.start()
    load_attn = pltpu.make_async_copy(attn_ref, attn, t_sem.at[3])
    load_attn.start()
    greet(others("seq", 8) + others("grp", 32))
    me, right, left, across, twin = neighbours()
    g = lax.axis_index("grp")

    place = onehot(iota((128, ROWS), 0) == pos_ref[...])
    j = iota((ROWS, ROWS), 1)
    turned = lax.rem(g + 32 - (j % PART // 2 * 2 + j // PART), 32) * 2 + j % 2
    place = mm(place, onehot(iota((ROWS, ROWS), 0) == turned)).astype(BF16)
    pick = mm_nt(eye(ROWS), place).astype(BF16)
    taken = jnp.sum(place.astype(F32), axis=1, keepdims=True) > 0.5
    load_a.wait()

    def vision_tile(n, k):
        d = lax.rem(me + k, 8)
        return remote(proj.at[n, d], vis.at[n, me], s1.at[n, k], r1.at[n, k], {"seq": d})

    def project(n, _):
        load_w(n).wait()
        cols = pl.ds(pl.multiple_of(n * 256, 256), 256)
        total = mm(a[...].reshape(512, MERGER_FEATURES), w[:, cols]).astype(BF16)
        for q in range(2):
            for d in range(8):
                row = PART * (8 * q + d)
                proj[n, d, q] = total[row : row + PART]
        for k in range(1, 8):
            vision_tile(n, k).start()
        vis[n, me] = proj[n, me]
        return 0

    lax.fori_loop(0, 4, project, 0)
    load_cot.wait()
    for c in range(8):
        for n in range(4):
            picked[n, c] = mm(pick, cot[:, 1024 * c + 256 * n : 1024 * c + 256 * n + 256]).astype(BF16)
    load_text.wait()

    def back_part(q, k):
        d = lax.rem(me + k, 8)
        return remote(back.at[q, d], ret.at[q, me], s2.at[q, k], r2.at[q, k], {"seq": d})

    def gains(c, n):
        return gain_ref[:, pl.ds(pl.multiple_of(c * 1024 + n * 256, 256), 256)]

    def text_squares(c, carry):
        t = text[:, pl.ds(pl.multiple_of(c * 1024, 1024), 1024)].astype(F32)
        return carry + jnp.sum(t * t, axis=1, keepdims=True)

    r_text = lax.rsqrt(lax.fori_loop(0, 8, text_squares, jnp.zeros((128, 1), F32)) / 8192.0 + EPS)

    def tile_sums(n, carry):
        for k in range(1, 8):
            vision_tile(n, k).wait_recv()

        def sums(c, carry):
            v = vis[n, c].reshape(ROWS, 256).astype(F32)
            gy = picked[n, c].astype(F32) * gains(c, n)
            return carry[0] + v * v, carry[1] + gy * v

        return lax.fori_loop(0, 8, sums, carry)

    zero = jnp.zeros((ROWS, 256), F32)
    squares, products = lax.fori_loop(0, 4, tile_sums, (zero, zero))
    r = lax.rsqrt(jnp.sum(squares, axis=1, keepdims=True) / 8192.0 + EPS)
    slope = r * r * (jnp.sum(products, axis=1, keepdims=True) / 8192.0)

    for q in range(2):
        rows = slice(PART * q, PART * q + PART)

        def grads(c, ref):
            for n in range(4):
                gy = picked[n, c, rows].astype(F32) * gains(c, n)
                grad = r[rows] * (gy - vis[n, c, q].astype(F32) * slope[rows])
                ref[:, 256 * n : 256 * n + 256] = grad.astype(BF16)

        def send(k, _):
            d = lax.rem(me + k, 8)
            grads(d, back.at[q, d])
            back_part(q, k).start()
            return 0

        lax.fori_loop(1, 8, send, 0)
        grads(me, ret.at[q, me])

    def hidden_out(c):
        cols = pl.ds(pl.multiple_of(c * 1024, 1024), 1024)
        return pltpu.make_async_copy(text.at[:, cols], hid_ref.at[:, cols], h_sem.at[c])

    def hidden(c):
        for n in range(4):
            cols = pl.ds(pl.multiple_of(c * 1024 + n * 256, 256), 256)
            gain = gains(c, n)
            rows = (vis[n, c].reshape(ROWS, 256).astype(F32) * r * gain).astype(BF16)
            own = (text[:, cols].astype(F32) * r_text * gain).astype(BF16)
            text[:, cols] = jnp.where(taken, mm(place, rows), own.astype(F32)).astype(BF16)
        hidden_out(c).start()

    core = lax.rem(me, 2)
    x = me // 2
    chip_right, chip_left, chip_across = lax.rem(x + 1, 4), lax.rem(x + 3, 4), lax.rem(x + 2, 4)
    upper, lower = pl.ds(0, 2), pl.ds(2, 2)

    def to_twin(u):
        return remote(terms.at[u, 1 - core], twin_terms.at[u], s3.at[0, u], r3.at[0, u], {"seq": twin})

    def far_right(u):
        return remote(
            terms.at[u, core, chip_across, upper], far.at[u, upper], s3.at[1, u], r3.at[1, u], {"seq": right}
        )

    def far_left(u):
        return remote(
            terms.at[u, core, chip_across, lower], far.at[u, lower], s3.at[2, u], r3.at[2, u], {"seq": left}
        )

    def near_right(u):
        return remote(terms.at[u, core, chip_right], near.at[u, 0], s3.at[3, u], r3.at[3, u], {"seq": right})

    def near_left(u):
        return remote(terms.at[u, core, chip_left], near.at[u, 1], s3.at[4, u], r3.at[4, u], {"seq": left})

    to_granule = onehot(sub_block_of_granule(iota((128, 128), 0)) == iota((128, 128), 1))

    def route_back(t, n):
        d = lax.rem(g + 32 - (2 * (t % 2 * 8 + n) + t // 2), 32)
        return remote(granules.at[t, n], arrived.at[g], s4.at[t, n], r4.at[t, n], {"grp": d})

    def send_back(t):
        rows = mm(to_granule, summed[t].reshape(128, HALF)).astype(BF16)
        granules[t] = rows.reshape(8, 16, HALF)
        if t == 0:
            arrived[g] = granules[0, 0]
        for n in range(1 if t == 0 else 0, 8):
            route_back(t, n).start()

    def step(i, _):
        for q in range(2):
            @pl.when(i == 4 * q)
            def _():
                for k in range(1, 8):
                    back_part(q, k).wait_recv()

        @pl.when(i < 8)
        def _():
            u = i
            rows = pl.ds(pl.multiple_of(lax.rem(u, 2) * 2560, 2560), 2560)
            own = pl.ds(pl.multiple_of(lax.rem(u // 2, 2) * 16, 16), 16)
            total = mm_nt(ret[u // 4, :, own, :].reshape(128, 1024), w[rows, :]).astype(BF16)
            for s in range(8):
                for b in range(4):
                    terms[u, s % 2, s // 2, b] = total[16 * s : 16 * s + 16, HALF * b : HALF * b + HALF]
            to_twin(u).start()
            hidden(u)

        @pl.when((i >= 1) & (i < 9))
        def _():
            u = i - 1
            to_twin(u).wait_recv()
            terms[u, core] = (terms[u, core].astype(F32) + twin_terms[u].astype(F32)).astype(BF16)
            far_right(u).start()
            far_left(u).start()

        @pl.when((i >= 2) & (i < 10))
        def _():
            u = i - 2
            far_right(u).wait_recv()
            terms[u, core, chip_right, upper] = (
                terms[u, core, chip_right, upper].astype(F32) + far[u, upper].astype(F32)
            ).astype(BF16)
            near_right(u).start()
            far_left(u).wait_recv()
            terms[u, core, chip_left, lower] = (
                terms[u, core, chip_left, lower].astype(F32) + far[u, lower].astype(F32)
            ).astype(BF16)
            near_left(u).start()

        @pl.when(i >= 3)
        def _():
            u = i - 3
            near_right(u).wait_recv()
            near_left(u).wait_recv()
            total = terms[u, core, x].astype(F32) + near[u, 0].astype(F32) + near[u, 1].astype(F32)
            summed[u // 2, lax.rem(u, 2)] = total.astype(BF16)

        for t in range(3):
            @pl.when(i == 2 * t + 4)
            def _():
                send_back(t)

        return 0

    lax.fori_loop(0, 11, step, 0)
    send_back(3)

    def settle(u, _):
        for copy in (to_twin(u), far_right(u), far_left(u), near_right(u), near_left(u)):
            copy.wait_send()
        hidden_out(u).wait()
        return 0

    lax.fori_loop(0, 8, settle, 0)
    for q in range(2):
        for k in range(1, 8):
            back_part(q, k).wait_send()
    for n in range(4):
        for k in range(1, 8):
            vision_tile(n, k).wait_send()
    load_attn.wait()
    xhat, rstd = normalize(attn[...].reshape(VISION_WIDTH, 256), eye(256))
    take = mm_nt(eye(512), granule_of_patch(slot_ref)).astype(BF16)
    for t in range(4):
        for n in range(1 if t == 0 else 0, 8):
            route_back(t, n).wait()
    grads = mm(take, arrived[...].reshape(512, HALF))
    gy = jnp.concatenate([grads[:256], grads[256:]], axis=1) * mgain_ref[...]
    mean = jnp.mean(gy, axis=1, keepdims=True)
    along = jnp.mean(gy * xhat, axis=1, keepdims=True)
    out_ref[...] = (rstd * (gy - mean - xhat * along)).astype(BF16)


def params(collective_id=None):
    if collective_id is None:
        return pltpu.CompilerParams(vmem_limit_bytes=48 * 2**20)
    return pltpu.CompilerParams(
        vmem_limit_bytes=58 * 2**20, collective_id=collective_id, has_side_effects=True
    )


def shaped(*shape, dtype=BF16):
    return jax.ShapeDtypeStruct(shape, dtype)


def buffer(*shape):
    return pltpu.VMEM(shape, BF16)


def body(
    queries,
    key_rows,
    values,
    segment_ids,
    merger_norm_gain,
    merge_weight,
    text_rows,
    token_gain,
    cotangent,
    send_slot,
    place_pos,
):
    w = lax.all_gather(merge_weight, "grp", axis=0, tiled=True)
    gain = merger_norm_gain.reshape(1, VISION_WIDTH)
    slot = send_slot.reshape(1, ROWS)

    x = pl.pallas_call(
        heads_out,
        out_shape=shaped(8, 496, 256),
        in_specs=[VMEM] * 4,
        out_specs=VMEM,
        scratch_shapes=[buffer(8, 496, 256), DMA((8,)), DMA((8,)), DMA(())],
        compiler_params=params(1),
        name="heads_out",
    )(queries, key_rows, values, segment_ids.reshape(1, 256))
    o = pl.pallas_call(
        attention,
        out_shape=shaped(8, 160, 256),
        in_specs=[VMEM],
        out_specs=VMEM,
        scratch_shapes=[
            pltpu.VMEM((8, 2, 256, HEAD_DIM), BF16),
            pltpu.VMEM((8, 256, 128), F32),
            pltpu.VMEM((2, 8, 256, 256), F32),
        ],
        compiler_params=params(),
        name="attention",
    )(x)
    attn, a = pl.pallas_call(
        merge_and_gather,
        out_shape=[shaped(8, 160, 256), shaped(2, 8, PART, MERGER_FEATURES)],
        in_specs=[VMEM] * 3,
        out_specs=[VMEM] * 2,
        scratch_shapes=[
            buffer(32, 16, HALF),
            buffer(2, 16, 16, HALF),
            DMA((8,)),
            DMA((8,)),
            DMA((2, 16)),
            DMA((2, 16)),
            DMA(()),
            DMA((9, 2, 2)),
            DMA((9, 2, 2)),
        ],
        compiler_params=params(2),
        name="merge_and_gather",
    )(o, gain, slot)
    return pl.pallas_call(
        language,
        out_shape=[shaped(128, 8192), shaped(256, VISION_WIDTH)],
        in_specs=[ANY] * 4 + [VMEM] * 2 + [ANY] + [VMEM] * 2,
        out_specs=[ANY, VMEM],
        scratch_shapes=[
            buffer(2, 8, PART, MERGER_FEATURES),
            buffer(MERGER_FEATURES, 1024),
            buffer(128, 8192),
            buffer(128, 8192),
            buffer(4, 8, ROWS, 256),
            buffer(4, 8, 2, PART, 256),
            buffer(4, 8, 2, PART, 256),
            buffer(2, 8, PART, 1024),
            buffer(2, 8, PART, 1024),
            buffer(8, 2, 4, 4, 16, HALF),
            buffer(8, 4, 4, 16, HALF),
            buffer(8, 4, 16, HALF),
            buffer(8, 2, 4, 16, HALF),
            buffer(4, 2, 4, 16, HALF),
            buffer(4, 8, 16, HALF),
            buffer(32, 16, HALF),
            DMA((4,)),
            DMA((4,)),
            DMA((4, 8)),
            DMA((4, 8)),
            DMA((2, 8)),
            DMA((2, 8)),
            DMA((5, 8)),
            DMA((5, 8)),
            DMA((4, 8)),
            DMA((4, 8)),
            DMA((8,)),
            buffer(8, 160, 256),
        ],
        compiler_params=params(3),
        name="language",
    )(
        a,
        w,
        text_rows,
        cotangent,
        token_gain.reshape(1, 8192),
        place_pos.reshape(1, ROWS),
        attn,
        gain,
        slot,
    )


def solution(mesh):
    in_specs = (
        P(("grp", "seq"), None),
        P(("grp", "seq"), None),
        P(("grp", "seq"), None),
        P(("grp", "seq")),
        P(),
        P("grp", "seq"),
        P(("grp", "seq"), None),
        P(),
        P(("grp", "seq"), None),
        P(("grp", "seq")),
        P(("grp", "seq")),
    )
    out_specs = (P(("grp", "seq"), None), P(("grp", "seq"), None))
    return jax.shard_map(body, mesh=mesh, in_specs=in_specs, out_specs=out_specs, check_vma=False)
```
